32 devices in a mesh: coarse: 4 (over y, x), fine: 8 (over z, core).
Axes of the slice: x: 2, y: 2, z: 4, core: 2. Of those that a mesh axis runs over, the one named last changes fastest.
Arguments:
- embeddings: bfloat16 [16384, 512], P(('coarse', 'fine')), may hold values from -64 to 64
- labels: int32 [16384, 1], P(('coarse', 'fine')), may hold values from 0 to 7; in each aligned block of 512 rows (0 to 511, 512 to 1023, ...) at most 128 rows name the same one
Outputs:
- max_similarity: float32 [16384], P(('coarse', 'fine'))
The draws below stay inside these ranges and needn't reach their ends.
Inputs may be any that keep to these rules, and one draw needn't show every extreme that they name: `labels`: among the rows of one device no label appears more than 128 times; on some device one label appears exactly 128 times.
All inputs are finite; a program needn't handle non-finite values. Where the reference program divides by a largest or mean magnitude, that divisor is 1e-20 or more.
Results may differ from the reference program's by a relative error of at most 0.00035.
The reference program's roundings to bfloat16 on the way count: a program that leaves them out, or rounds other values in their place, can miss the bound.
Values may be sent and summed in bfloat16 or wider, within the bound.
A program may use at most 64 MiB of HBM per device.

```python
import math
import jax
import jax.numpy as jnp
import numpy as np
from jax import lax

D = 512
ROW_DEV = 512
ITERS = 2
ROWS = 16384
GROUP_ROWS = 4096
CAP = 128
N_COARSE = 4
N_FINE = 8


def draw_embeddings(key, part):
    keys = jax.random.split(key, 7)
    row_pos = (jnp.arange(ROWS, dtype=jnp.float32) / ROWS)[:, None]
    column_phase = jax.random.uniform(keys[0], (D,), jnp.float32, 0.0, 2.0 * math.pi)
    column_scale = jnp.exp(0.8 * jnp.cos(column_phase[None, :] + math.pi * row_pos))
    first_mean = jnp.clip(jax.random.normal(keys[1], (D,), jnp.float32), -3.0, 3.0)
    second_mean = jnp.clip(jax.random.normal(keys[2], (D,), jnp.float32), -3.0, 3.0)
    noise = jnp.clip(jax.random.normal(keys[3], (ROWS, D), jnp.float32), -4.0, 4.0)
    row_scale = jnp.exp(jax.random.uniform(keys[4], (ROWS, 1), jnp.float32, 0.0, math.log(10.0)))
    strength = 0.7
    heavy_device = jax.random.randint(keys[5], (), 0, ROWS // ROW_DEV)
    row_device = (jnp.arange(ROWS, dtype=jnp.int32) // ROW_DEV)[:, None]
    on_heavy = (row_device == heavy_device).astype(jnp.float32)
    boosted = (jax.random.randint(keys[6], (1, D), 0, 4) == 0).astype(jnp.float32)
    row_scale = row_scale * (1.0 - on_heavy) + 4.0 * on_heavy
    column_boost = 1.0 + 4.0 * on_heavy * boosted
    mixed = column_scale * column_boost * noise
    mixed = mixed + 0.6 * jnp.roll(mixed, 1, axis=1)
    common = strength * (first_mean[None, :] * jnp.cos(math.pi * row_pos) + second_mean[None, :] * jnp.sin(math.pi * row_pos))
    values = jnp.clip(row_scale * (mixed + common), -64.0, 64.0)
    return values.astype(jnp.bfloat16)


def shared_out(key, own, number, rows, amount, top, limit, slope):
    order = jax.random.permutation(key, amount)
    heavy_load, usual = load_shares(amount, rows * top, limit, slope, True), load_shares(amount, rows * top, limit, slope, False)
    places = jnp.arange(amount)

    def named(lengths, turn):
        used = int((lengths > 0).sum())
        fixed = max(1, used // 4)
        passed = fixed + (places - fixed + turn * (used - fixed)) % max(1, amount - fixed)
        return jnp.zeros((amount,), jnp.int32).at[order[jnp.where(places < fixed, places, passed)]].set(jnp.asarray(lengths, jnp.int32))

    lengths = jnp.where(number % 4 == 0, named(heavy_load, number // 4), named(usual, number - number // 4 - 1))
    mixed = jax.random.permutation(jax.random.fold_in(own, 3), amount)
    source_of, receiver = mixed[0:amount // 2 * 2:2], mixed[1:amount // 2 * 2:2]
    margin = jnp.minimum(lengths[source_of] - 1, limit - lengths[receiver]) // 2
    margin = jnp.where((source_of == order[0]) | (receiver == order[0]) | (lengths[receiver] == 0), 0, jnp.maximum(margin, 0))
    passed = jax.random.randint(jax.random.fold_in(own, 4), (amount // 2,), 0, 1 << 20) % (margin + 1)
    lengths = lengths.at[source_of].add(-passed).at[receiver].add(passed)
    items = jnp.searchsorted(jnp.cumsum(lengths), jnp.arange(rows * top), side="right").astype(jnp.int32)
    table = items.reshape(top, rows).T
    table = table[jax.random.permutation(jax.random.fold_in(own, 1), rows)]
    turn = jax.random.randint(jax.random.fold_in(own, 2), (rows, 1), 0, top)
    return jnp.take_along_axis(table, (jnp.arange(top)[None, :] + turn) % top, axis=1)


def load_shares(number_of, total, most, slope, full):
    portions = [(1 << 20) // math.isqrt(rank ** slope) + 1 for rank in range(1, number_of + 1)]
    largest = most if full else min(most, max(-(-total // number_of), total * portions[0] // sum(portions)))
    least = 1 if total - largest >= number_of - 1 else 0
    given, surplus = [largest] + [least] * (number_of - 1), total - largest - least * (number_of - 1)
    while surplus > 0:
        candidates = [i for i in range(1, number_of) if given[i] < largest] or [i for i in range(1, number_of) if given[i] < most]
        mass, left = sum([portions[i] for i in candidates]), surplus
        for i in candidates:
            addition = min(most - given[i], max(1, left * portions[i] // mass), surplus)
            given[i] = given[i] + addition
            surplus = surplus - addition
    return np.array(given)


def setup_inputs(seed: int = 0) -> dict:
    splits = jax.random.split(jax.random.key(seed), 3)
    embeddings = draw_embeddings(jax.random.fold_in(splits[2], 71), 0)
    labels_keys = jax.random.split(jax.random.fold_in(splits[1], 1), ROWS // ROW_DEV)
    labels_turns = jax.random.permutation(jax.random.fold_in(splits[1], 3), ROWS // ROW_DEV)
    labels = jax.vmap(lambda own, number: shared_out(jax.random.fold_in(splits[1], 2), own, number, ROW_DEV, N_FINE, 1, CAP, 2))(labels_keys, labels_turns).reshape((ROWS, 1))
    return dict(embeddings=embeddings, labels=labels)


EPS = 1e-06
RIDGE = 0.001

def matmul_high(left, right):
    return jnp.dot(left, right, precision=lax.Precision.HIGHEST, preferred_element_type=jnp.float32)

def inverse_root(second):
    identity = jnp.eye(second.shape[0], dtype=jnp.float32)
    norm_scale = jnp.max(lax.optimization_barrier(jnp.sum(jnp.abs(second), axis=1)))
    root_est = second / norm_scale
    inverse_est = identity
    for sweep in range(ITERS):
        newton_step = 0.5 * (3.0 * identity - matmul_high(inverse_est, root_est))
        root_est = matmul_high(root_est, newton_step)
        inverse_est = matmul_high(newton_step, inverse_est)
    return (inverse_est / jnp.sqrt(norm_scale)).astype(jnp.bfloat16)

def unit_rows(values, whiten_b):
    whitened = jnp.dot(values, whiten_b, preferred_element_type=jnp.float32)
    width_value = whitened.shape[-1]
    meansq = lax.optimization_barrier(jnp.mean(whitened * whitened, axis=-1, keepdims=True))
    return (whitened * lax.rsqrt(width_value * (meansq + EPS))).astype(jnp.bfloat16)

def label_best(pieces):
    buffer_rows, valid_slots = pieces
    similar = jnp.dot(buffer_rows, buffer_rows.T, preferred_element_type=jnp.float32)
    slot_total = buffer_rows.shape[0]
    keep_mask = (valid_slots[None, :] > 0) & jnp.logical_not(jnp.eye(slot_total, dtype=bool))
    return lax.optimization_barrier(jnp.max(jnp.where(keep_mask, similar, -1.0), axis=1))

def reference(embeddings, labels):
    second = lax.dot_general(embeddings, embeddings, (((0,), (0,)), ((), ())), preferred_element_type=jnp.float32)
    second = second / ROWS + RIDGE * jnp.eye(D, dtype=jnp.float32)
    whiten_b = inverse_root(second)
    grouped = embeddings.reshape(N_COARSE, GROUP_ROWS, D)
    group_labels = labels.reshape(N_COARSE, N_FINE, ROW_DEV)

    def group_best(pieces):
        group_rows, owner_label = pieces
        unit_values = unit_rows(group_rows, whiten_b)
        onehot = (owner_label[..., None] == jnp.arange(N_FINE, dtype=jnp.int32)).astype(jnp.int32)
        rank_before = jnp.cumsum(onehot, axis=1, dtype=jnp.int32) - onehot
        slot_index = lax.optimization_barrier(jnp.sum(rank_before * onehot, axis=2)).astype(jnp.int32)
        source = jnp.arange(N_FINE, dtype=jnp.int32)[:, None]
        position = (source * CAP + slot_index).reshape(-1).astype(jnp.int32)
        flat_label = owner_label.reshape(-1).astype(jnp.int32)
        buffers = jnp.zeros((N_FINE, N_FINE * CAP, D), jnp.bfloat16).at[flat_label, position].set(unit_values)
        valid_slots = jnp.zeros((N_FINE, N_FINE * CAP), jnp.float32).at[flat_label, position].set(1.0)
        best_match = lax.map(label_best, (buffers, valid_slots))
        return best_match[flat_label, position]
    return lax.map(group_best, (grouped, group_labels)).reshape(ROWS)
```

```python
import functools

import jax
import jax.numpy as jnp
from jax import lax
from jax.experimental import pallas as pl
from jax.experimental.pallas import tpu as pltpu
from jax.sharding import PartitionSpec as P

EPS = 1e-06
RIDGE = 0.001
LANES = 128
LOW = -3.0e38
MESH = pl.DeviceIdType.MESH


def dot(left, right):
    return jnp.dot(left, right, preferred_element_type=jnp.float32)


def split_two(value):
    high = value.astype(jnp.bfloat16)
    return high, (value - high.astype(jnp.float32)).astype(jnp.bfloat16)


def dot_split(left, right):
    left_high, left_low = left
    right_high, right_low = right
    return dot(left_high, right_high) + (dot(left_high, right_low) + dot(left_low, right_high))


def remote(src, dst, send_sem, recv_sem, device):
    return pltpu.make_async_remote_copy(
        src_ref=src, dst_ref=dst, send_sem=send_sem, recv_sem=recv_sem,
        device_id=device, device_id_type=MESH,
    )


def rows_at(ref, start, size):
    return ref.at[pl.ds(pl.multiple_of(start, 8), size)]


def kernel(
    C, F, slot, stack_rows, row_total,
    emb, labels, out,
    acc, half_in, half, coarse_in, part, z_in, total,
    outgoing, received, counts_out, counts_in, full, whiten, unit, bias, best, returned,
    core_s, core_r, coarse_s, coarse_r, z_s, z_r, gz_s, gz_r, gc_s, gc_r, gk_s, gk_r,
    a_s, a_r, n_s, n_r, b_s, b_r,
):
    rows, width = emb.shape
    blocks = width // LANES
    pairs = [(i, j) for i in range(blocks) for j in range(i, blocks)]
    Z = F // 2
    slots = F * slot
    c = lax.axis_index("coarse")
    f = lax.axis_index("fine")
    core = lax.rem(f, 2)
    z = lax.div(f, 2)
    sibling = (c, f + 1 - 2 * core)

    def fine_peer(k):
        return lax.rem(f + k, F)

    def coarse_peer(k):
        return lax.rem(c + k, C)

    def z_peer(k):
        return lax.rem(z + k, Z)

    barrier = pltpu.get_barrier_semaphore()
    for k in range(1, F):
        pl.semaphore_signal(barrier, inc=1, device_id=(c, fine_peer(k)), device_id_type=MESH)
    for k in range(1, C):
        pl.semaphore_signal(barrier, inc=1, device_id=(coarse_peer(k), f), device_id_type=MESH)

    used = len(pairs) * LANES
    if stack_rows > used:
        acc[used:, :] = jnp.zeros((stack_rows - used, LANES), jnp.float32)
    place = 0
    for i in range(blocks):
        strip = lax.dot_general(
            emb[:, i * LANES:(i + 1) * LANES], emb[:, i * LANES:],
            (((0,), (0,)), ((), ())), preferred_element_type=jnp.float32,
        )
        for j in range(blocks - i):
            acc[place * LANES:(place + 1) * LANES, :] = strip[:, j * LANES:(j + 1) * LANES]
            place += 1
    pl.semaphore_wait(barrier, F + C - 2)

    half_rows = stack_rows // 2
    part_rows = half_rows // C
    piece_rows = part_rows // Z

    core_copy = remote(
        rows_at(acc, (1 - core) * half_rows, half_rows), half_in, core_s, core_r, sibling
    )
    core_copy.start()

    label_row = labels[...]
    onehot = lax.broadcasted_iota(jnp.int32, (F, rows), 0) == label_row
    before = (
        lax.broadcasted_iota(jnp.int32, (rows, rows), 0)
        < lax.broadcasted_iota(jnp.int32, (rows, rows), 1)
    )
    flags = jnp.where(onehot, 1.0, 0.0)
    rank_all = dot(flags.astype(jnp.bfloat16), jnp.where(before, 1.0, 0.0).astype(jnp.bfloat16))
    rank = jnp.sum(jnp.where(onehot, rank_all, 0.0), axis=0, keepdims=True).astype(jnp.int32)
    amounts = jnp.sum(flags, axis=1, keepdims=True)
    for label in range(F):
        counts_out[label] = jnp.broadcast_to(amounts[label:label + 1, :], (8, LANES))
    slot_of = label_row * slot + rank
    step = min(256, slots)
    for start in range(0, slots, step):
        pick = lax.broadcasted_iota(jnp.int32, (step, rows), 0) + start == slot_of
        outgoing[start:start + step, :] = dot(
            jnp.where(pick, 1.0, 0.0).astype(jnp.bfloat16), emb[...]
        ).astype(jnp.bfloat16)

    def slot_rows(ref, which):
        return ref.at[pl.ds(pl.multiple_of(which * slot, 16), slot)]

    def row_copy(to, source):
        return remote(
            slot_rows(outgoing, to), slot_rows(received, source), a_s.at[to], a_r.at[source], (c, to)
        )

    def count_copy(to, source):
        return remote(counts_out.at[to], counts_in.at[source], n_s.at[to], n_r.at[source], (c, to))

    for k in range(1, F):
        count_copy(fine_peer(k), f).start()

    core_copy.wait_recv()
    half[...] = rows_at(acc, core * half_rows, half_rows)[...] + half_in[...]

    def coarse_copy(to, source):
        return remote(
            rows_at(half, to * part_rows, part_rows), coarse_in.at[source],
            coarse_s.at[to], coarse_r.at[source], (to, f),
        )

    for k in range(1, C):
        coarse_copy(coarse_peer(k), c).start()
    for k in range(1, F):
        row_copy(fine_peer(k), f).start()
    value = rows_at(half, c * part_rows, part_rows)[...]
    for k in range(1, C):
        coarse_copy(coarse_peer(k), coarse_peer(k)).wait_recv()
        value = value + coarse_in[coarse_peer(k)]
    part[...] = value

    def z_copy(to, source):
        return remote(
            rows_at(part, to * piece_rows, piece_rows), z_in.at[source],
            z_s.at[to], z_r.at[source], (c, 2 * to + core),
        )

    for k in range(1, Z):
        z_copy(z_peer(k), z).start()
    value = rows_at(part, z * piece_rows, piece_rows)[...]
    for k in range(1, Z):
        z_copy(z_peer(k), z_peer(k)).wait_recv()
        value = value + z_in[z_peer(k)]

    def piece_start(coarse_id, z_id):
        return core * half_rows + coarse_id * part_rows + z_id * piece_rows

    rows_at(total, piece_start(c, z), piece_rows)[...] = value

    def z_gather(to, source):
        piece = rows_at(total, piece_start(c, source), piece_rows)
        return remote(piece, piece, gz_s.at[to], gz_r.at[source], (c, 2 * to + core))

    def coarse_gather(to, source):
        piece = rows_at(total, piece_start(source, 0), part_rows)
        return remote(piece, piece, gc_s.at[to], gc_r.at[source], (to, f))

    def core_gather(source):
        piece = rows_at(total, source * half_rows, half_rows)
        return remote(piece, piece, gk_s, gk_r, sibling)

    for k in range(1, Z):
        z_gather(z_peer(k), z).start()
    for k in range(1, Z):
        z_gather(z_peer(k), z_peer(k)).wait_recv()
    for k in range(1, C):
        coarse_gather(coarse_peer(k), c).start()
    for k in range(1, C):
        coarse_gather(coarse_peer(k), coarse_peer(k)).wait_recv()
    core_gather(core).start()

    slot_rows(received, f)[...] = slot_rows(outgoing, f)[...]
    counts_in[f] = counts_out[f]
    for k in range(1, F):
        count_copy(fine_peer(k), fine_peer(k)).wait_recv()
    rank_here = lax.broadcasted_iota(jnp.int32, (slot, LANES), 0).astype(jnp.float32)
    for source in range(F):
        bias[source * slot:(source + 1) * slot, :] = jnp.where(
            rank_here < counts_in[source][0:1, :], 0.0, LOW
        )

    core_gather(1 - core).wait_recv()
    for place, (i, j) in enumerate(pairs):
        block = total[place * LANES:(place + 1) * LANES, :] / row_total
        if i == j:
            diagonal = (
                lax.broadcasted_iota(jnp.int32, (LANES, LANES), 0)
                == lax.broadcasted_iota(jnp.int32, (LANES, LANES), 1)
            )
            block = block + jnp.where(diagonal, RIDGE, 0.0)
        else:
            full[j * LANES:(j + 1) * LANES, i * LANES:(i + 1) * LANES] = block.T
        full[i * LANES:(i + 1) * LANES, j * LANES:(j + 1) * LANES] = block
    second = full[...]
    norm_scale = jnp.max(jnp.sum(jnp.abs(second), axis=0, keepdims=True), axis=1, keepdims=True)
    root = second / norm_scale
    identity = jnp.where(
        lax.broadcasted_iota(jnp.int32, (width, width), 0)
        == lax.broadcasted_iota(jnp.int32, (width, width), 1),
        1.0, 0.0,
    )
    root_parts = split_two(root)
    square = dot_split(root_parts, root_parts)
    outer = 1.6875 * identity - 0.5625 * root + 0.0625 * square
    inverse = 2.25 * identity - 2.4375 * root + dot_split(split_two(square), split_two(outer))
    whiten[...] = (inverse / jnp.sqrt(norm_scale)).astype(jnp.bfloat16)

    for k in range(1, F):
        row_copy(fine_peer(k), fine_peer(k)).wait_recv()
    chunk = LANES
    for start in range(0, slots, chunk):
        white = dot(received[start:start + chunk, :], whiten[...])
        meansq = jnp.mean(white * white, axis=-1, keepdims=True)
        unit[start:start + chunk, :] = (white * lax.rsqrt(width * (meansq + EPS))).astype(jnp.bfloat16)

    diagonal = (
        lax.broadcasted_iota(jnp.int32, (LANES, LANES), 0)
        == lax.broadcasted_iota(jnp.int32, (LANES, LANES), 1)
    )
    tops = [jnp.full((8, LANES), -1.0, jnp.float32) for _ in range(slots // LANES)]
    for start in range(0, slots, chunk):
        similar = lax.dot_general(
            unit[start:start + chunk, :], unit[...], (((1,), (1,)), ((), ())),
            preferred_element_type=jnp.float32,
        )
        weight = bias[start:start + chunk, :]
        for t in range(slots // LANES):
            tile = similar[:, t * LANES:(t + 1) * LANES] + weight
            if t * LANES == start:
                tile = jnp.where(diagonal, LOW, tile)
            tops[t] = jnp.maximum(tops[t], jnp.max(tile.reshape(chunk // 8, 8, LANES), axis=0))
    for t in range(slots // LANES):
        best[t] = jnp.broadcast_to(jnp.max(tops[t], axis=0, keepdims=True), (8, LANES))

    def best_copy(to, source):
        return remote(
            best.at[lax.div(to * slot, LANES)], returned.at[source], b_s.at[to], b_r.at[source], (c, to)
        )

    for k in range(1, F):
        best_copy(fine_peer(k), f).start()
    returned[f] = best[lax.div(f * slot, LANES)]
    pick = lax.broadcasted_iota(jnp.int32, (LANES, rows), 0) == rank + lax.rem(f * slot, LANES)
    pick = jnp.where(pick, 1.0, 0.0).astype(jnp.bfloat16)
    mine = lax.broadcasted_iota(jnp.int32, (F * 8, rows), 0) == label_row * 8
    for k in range(1, F):
        best_copy(fine_peer(k), fine_peer(k)).wait_recv()
    values = returned[...].reshape(F * 8, LANES)
    high, rest = values.astype(jnp.bfloat16), None
    rest = values - high.astype(jnp.float32)
    middle, low = split_two(rest)
    found = dot(high, pick) + (dot(middle, pick) + dot(low, pick))
    out[...] = jnp.sum(jnp.where(mine, found, 0.0), axis=0, keepdims=True)

    core_copy.wait_send()
    core_gather(core).wait_send()
    for k in range(1, C):
        coarse_copy(coarse_peer(k), c).wait_send()
        coarse_gather(coarse_peer(k), c).wait_send()
    for k in range(1, Z):
        z_copy(z_peer(k), z).wait_send()
        z_gather(z_peer(k), z).wait_send()
    for k in range(1, F):
        row_copy(fine_peer(k), f).wait_send()
        count_copy(fine_peer(k), f).wait_send()
        best_copy(fine_peer(k), f).wait_send()


def per_device(embeddings, labels):
    rows, width = embeddings.shape
    F = lax.axis_size("fine")
    C = lax.axis_size("coarse")
    Z = F // 2
    slot = 2 * rows // F
    slots = F * slot
    blocks = width // LANES
    unit_rows = 8 * C * F
    stack_rows = -(-(blocks * (blocks + 1) // 2 * LANES) // unit_rows) * unit_rows
    half_rows = stack_rows // 2
    part_rows = half_rows // C
    piece_rows = part_rows // Z
    f32, bf16 = jnp.float32, jnp.bfloat16
    dma = pltpu.SemaphoreType.DMA
    best = pl.pallas_call(
        functools.partial(kernel, C, F, slot, stack_rows, rows * F * C),
        out_shape=jax.ShapeDtypeStruct((1, rows), f32),
        in_specs=[pl.BlockSpec(memory_space=pltpu.VMEM)] * 2,
        out_specs=pl.BlockSpec(memory_space=pltpu.VMEM),
        scratch_shapes=[
            pltpu.VMEM((stack_rows, LANES), f32),
            pltpu.VMEM((half_rows, LANES), f32),
            pltpu.VMEM((half_rows, LANES), f32),
            pltpu.VMEM((C, part_rows, LANES), f32),
            pltpu.VMEM((part_rows, LANES), f32),
            pltpu.VMEM((Z, piece_rows, LANES), f32),
            pltpu.VMEM((stack_rows, LANES), f32),
            pltpu.VMEM((slots, width), bf16),
            pltpu.VMEM((slots, width), bf16),
            pltpu.VMEM((F, 8, LANES), f32),
            pltpu.VMEM((F, 8, LANES), f32),
            pltpu.VMEM((width, width), f32),
            pltpu.VMEM((width, width), bf16),
            pltpu.VMEM((slots, width), bf16),
            pltpu.VMEM((slots, LANES), f32),
            pltpu.VMEM((slots // LANES, 8, LANES), f32),
            pltpu.VMEM((F, 8, LANES), f32),
            dma, dma, dma((C,)), dma((C,)), dma((Z,)), dma((Z,)),
            dma((Z,)), dma((Z,)), dma((C,)), dma((C,)), dma, dma,
            dma((F,)), dma((F,)), dma((F,)), dma((F,)), dma((F,)), dma((F,)),
        ],
        compiler_params=pltpu.CompilerParams(
            collective_id=0, has_side_effects=True, vmem_limit_bytes=48 * 1024 * 1024
        ),
    )(embeddings, labels.reshape(1, rows))
    return best.reshape(rows)


def solution(mesh):
    in_specs = (P(("coarse", "fine"), None), P(("coarse", "fine"), None))
    out_specs = P(("coarse", "fine"))
    return jax.shard_map(
        per_device, mesh=mesh, in_specs=in_specs, out_specs=out_specs, check_vma=False
    )
```

```python
import functools

import jax
import jax.numpy as jnp
from jax import lax
from jax.experimental import pallas as pl
from jax.experimental.pallas import tpu as pltpu
from jax.sharding import PartitionSpec as P

EPS = 1e-06
RIDGE = 0.001
LANES = 128
LOW = -3.0e38
MESH = pl.DeviceIdType.MESH


def dot(left, right):
    return jnp.dot(left, right, preferred_element_type=jnp.float32)


def split_two(value):
    high = value.astype(jnp.bfloat16)
    return high, (value - high.astype(jnp.float32)).astype(jnp.bfloat16)


def dot_split(left, right):
    left_high, left_low = left
    right_high, right_low = right
    return dot(left_high, right_high) + (dot(left_high, right_low) + dot(left_low, right_high))


def remote(src, dst, send_sem, recv_sem, device):
    return pltpu.make_async_remote_copy(
        src_ref=src, dst_ref=dst, send_sem=send_sem, recv_sem=recv_sem,
        device_id=device, device_id_type=MESH,
    )


def rows_at(ref, start, size):
    return ref.at[pl.ds(pl.multiple_of(start, 8), size)]


def kernel(
    C, F, slot, stack_rows, row_total,
    emb_hbm, labels_hbm, out,
    emb, labels, acc, half_in, half, coarse_in, part, z_in, total,
    outgoing, received, counts_out, counts_in, full, whiten, unit, best, returned,
    emb_sem, labels_sem,    core_s, core_r, coarse_s, coarse_r, z_s, z_r, gz_s, gz_r, gc_s, gc_r, gk_s, gk_r,
    a_s, a_r, n_s, n_r, b_s, b_r,
):
    emb_copy = pltpu.make_async_copy(emb_hbm, emb, emb_sem)
    labels_copy = pltpu.make_async_copy(labels_hbm, labels, labels_sem)
    emb_copy.start()
    labels_copy.start()
    rows, width = emb.shape
    blocks = width // LANES
    pairs = [(i, j) for i in range(blocks) for j in range(i, blocks)]
    Z = F // 2
    slots = F * slot
    c = lax.axis_index("coarse")
    f = lax.axis_index("fine")
    core = lax.rem(f, 2)
    z = lax.div(f, 2)
    sibling = (c, f + 1 - 2 * core)

    def fine_peer(k):
        return lax.rem(f + k, F)

    def coarse_peer(k):
        return lax.rem(c + k, C)

    def z_peer(k):
        return lax.rem(z + k, Z)

    def z_other(k, flip):
        return 2 * z_peer(k) + (1 - core if flip else core)

    steps = sorted(range(1, Z), key=lambda k: -min(k, Z - k))
    first = [z_other(k, False) for k in steps] + [z_other(0, True)]
    second_lot = [z_other(k, True) for k in steps]
    peers = first + second_lot

    barrier = pltpu.get_barrier_semaphore()
    for k in range(1, F):
        pl.semaphore_signal(barrier, inc=1, device_id=(c, fine_peer(k)), device_id_type=MESH)
    for k in range(1, C):
        pl.semaphore_signal(barrier, inc=1, device_id=(coarse_peer(k), f), device_id_type=MESH)

    emb_copy.wait()
    used = len(pairs) * LANES
    if stack_rows > used:
        acc[used:, :] = jnp.zeros((stack_rows - used, LANES), jnp.float32)
    place = 0
    for i in range(blocks):
        strip = lax.dot_general(
            emb[:, i * LANES:(i + 1) * LANES], emb[:, i * LANES:],
            (((0,), (0,)), ((), ())), preferred_element_type=jnp.float32,
        )
        for j in range(blocks - i):
            acc[place * LANES:(place + 1) * LANES, :] = strip[:, j * LANES:(j + 1) * LANES]
            place += 1
    pl.semaphore_wait(barrier, F + C - 2)

    half_rows = stack_rows // 2
    part_rows = half_rows // C
    piece_rows = part_rows // Z

    core_copy = remote(
        rows_at(acc, (1 - core) * half_rows, half_rows), half_in, core_s, core_r, sibling
    )
    core_copy.start()

    labels_copy.wait()
    label_row = labels[...]
    onehot = lax.broadcasted_iota(jnp.int32, (F, rows), 0) == label_row
    before = (
        lax.broadcasted_iota(jnp.int32, (rows, rows), 0)
        < lax.broadcasted_iota(jnp.int32, (rows, rows), 1)
    )
    flags = jnp.where(onehot, 1.0, 0.0)
    rank_all = dot(flags.astype(jnp.bfloat16), jnp.where(before, 1.0, 0.0).astype(jnp.bfloat16))
    rank = jnp.sum(jnp.where(onehot, rank_all, 0.0), axis=0, keepdims=True).astype(jnp.int32)
    amounts = jnp.sum(flags, axis=1, keepdims=True)
    for label in range(F):
        counts_out[label] = jnp.broadcast_to(amounts[label:label + 1, :], (8, LANES))
    slot_of = label_row * slot + rank
    step = min(256, slots)
    for start in range(0, slots, step):
        pick = lax.broadcasted_iota(jnp.int32, (step, rows), 0) + start == slot_of
        outgoing[start:start + step, :] = dot(
            jnp.where(pick, 1.0, 0.0).astype(jnp.bfloat16), emb[...]
        ).astype(jnp.bfloat16)

    def slot_rows(ref, which):
        return ref.at[pl.ds(pl.multiple_of(which * slot, 16), slot)]

    def row_copy(to, source):
        return remote(
            slot_rows(outgoing, to), slot_rows(received, source), a_s.at[to], a_r.at[source], (c, to)
        )

    def count_copy(to, source):
        return remote(counts_out.at[to], counts_in.at[source], n_s.at[to], n_r.at[source], (c, to))

    for k in range(1, F):
        count_copy(fine_peer(k), f).start()

    core_copy.wait_recv()
    half[...] = rows_at(acc, core * half_rows, half_rows)[...] + half_in[...]

    def coarse_copy(to, source):
        return remote(
            rows_at(half, to * part_rows, part_rows), coarse_in.at[source],
            coarse_s.at[to], coarse_r.at[source], (to, f),
        )

    for k in range(1, C):
        coarse_copy(coarse_peer(k), c).start()
    for peer in first:
        row_copy(peer, f).start()
    value = rows_at(half, c * part_rows, part_rows)[...]
    for k in range(1, C):
        coarse_copy(coarse_peer(k), coarse_peer(k)).wait_recv()
        value = value + coarse_in[coarse_peer(k)]
    part[...] = value

    def z_copy(to, source):
        return remote(
            rows_at(part, to * piece_rows, piece_rows), z_in.at[source],
            z_s.at[to], z_r.at[source], (c, 2 * to + core),
        )

    for k in range(1, Z):
        z_copy(z_peer(k), z).start()
    value = rows_at(part, z * piece_rows, piece_rows)[...]
    for k in range(1, Z):
        z_copy(z_peer(k), z_peer(k)).wait_recv()
        value = value + z_in[z_peer(k)]

    def piece_start(coarse_id, z_id):
        return core * half_rows + coarse_id * part_rows + z_id * piece_rows

    rows_at(total, piece_start(c, z), piece_rows)[...] = value

    def z_gather(to, source):
        piece = rows_at(total, piece_start(c, source), piece_rows)
        return remote(piece, piece, gz_s.at[to], gz_r.at[source], (c, 2 * to + core))

    def coarse_gather(to, source):
        piece = rows_at(total, piece_start(source, 0), part_rows)
        return remote(piece, piece, gc_s.at[to], gc_r.at[source], (to, f))

    def core_gather(source):
        piece = rows_at(total, source * half_rows, half_rows)
        return remote(piece, piece, gk_s, gk_r, sibling)

    for k in range(1, Z):
        z_gather(z_peer(k), z).start()
    for peer in second_lot:
        row_copy(peer, f).start()
    for k in range(1, Z):
        z_gather(z_peer(k), z_peer(k)).wait_recv()
    for k in range(1, C):
        coarse_gather(coarse_peer(k), c).start()
    for k in range(1, C):
        coarse_gather(coarse_peer(k), coarse_peer(k)).wait_recv()
    core_gather(core).start()

    slot_rows(received, f)[...] = slot_rows(outgoing, f)[...]
    counts_in[f] = counts_out[f]
    for k in range(1, F):
        count_copy(fine_peer(k), fine_peer(k)).wait_recv()

    core_gather(1 - core).wait_recv()
    for place, (i, j) in enumerate(pairs):
        block = total[place * LANES:(place + 1) * LANES, :] / row_total
        if i == j:
            diagonal = (
                lax.broadcasted_iota(jnp.int32, (LANES, LANES), 0)
                == lax.broadcasted_iota(jnp.int32, (LANES, LANES), 1)
            )
            block = block + jnp.where(diagonal, RIDGE, 0.0)
        else:
            full[j * LANES:(j + 1) * LANES, i * LANES:(i + 1) * LANES] = block.T
        full[i * LANES:(i + 1) * LANES, j * LANES:(j + 1) * LANES] = block
    second = full[...]
    norm_scale = jnp.max(jnp.sum(jnp.abs(second), axis=0, keepdims=True), axis=1, keepdims=True)
    root = second / norm_scale
    identity = jnp.where(
        lax.broadcasted_iota(jnp.int32, (width, width), 0)
        == lax.broadcasted_iota(jnp.int32, (width, width), 1),
        1.0, 0.0,
    )
    root_parts = split_two(root)
    square = dot_split(root_parts, root_parts)
    outer = 1.6875 * identity - 0.5625 * root + 0.0625 * square
    inverse = 2.25 * identity - 2.4375 * root + dot_split(split_two(square), split_two(outer))
    whiten[...] = (inverse / jnp.sqrt(norm_scale)).astype(jnp.bfloat16)

    group = LANES // slot
    if group == 1:
        order = [f] + peers
    else:
        order = [lax.rem(lax.div(f, group) + n, F // group) for n in range(F // group)]
        for peer in peers:
            row_copy(peer, peer).wait_recv()
    rank_here = lax.broadcasted_iota(jnp.int32, (slot, LANES), 0).astype(jnp.float32)
    diagonal = (
        lax.broadcasted_iota(jnp.int32, (LANES, LANES), 0)
        == lax.broadcasted_iota(jnp.int32, (LANES, LANES), 1)
    )

    def highest(tile):
        return jnp.max(tile.reshape(LANES // 8, 8, LANES), axis=0)

    tops, biases = [], []
    for n, block in enumerate(order):
        if group == 1 and n > 0:
            row_copy(block, block).wait_recv()
        white = dot(rows_at(received, block * LANES, LANES)[...], whiten[...])
        meansq = jnp.mean(white * white, axis=-1, keepdims=True)
        here = (white * lax.rsqrt(width * (meansq + EPS))).astype(jnp.bfloat16)
        unit[n * LANES:(n + 1) * LANES, :] = here
        bias = [
            jnp.where(rank_here < counts_in[block * group + m][0:1, :], 0.0, LOW) for m in range(group)
        ]
        bias = bias[0] if group == 1 else jnp.concatenate(bias, axis=0)
        so_far = unit[0:(n + 1) * LANES, :]
        down = lax.dot_general(here, so_far, (((1,), (1,)), ((), ())), preferred_element_type=jnp.float32)
        for t in range(n):
            tops[t] = jnp.maximum(tops[t], highest(down[:, t * LANES:(t + 1) * LANES] + bias))
        top = highest(jnp.where(diagonal, LOW, down[:, n * LANES:] + bias))
        if n > 0:
            across = lax.dot_general(
                unit[0:n * LANES, :], here, (((1,), (1,)), ((), ())), preferred_element_type=jnp.float32
            )
            for t in range(n):
                top = jnp.maximum(top, highest(across[t * LANES:(t + 1) * LANES, :] + biases[t]))
        tops.append(jnp.maximum(top, -1.0))
        biases.append(bias)
    for n, block in enumerate(order):
        best[block] = jnp.broadcast_to(jnp.max(tops[n], axis=0, keepdims=True), (8, LANES))

    def best_copy(to, source):
        return remote(
            best.at[lax.div(to, group)], returned.at[source], b_s.at[to], b_r.at[source], (c, to)
        )

    for peer in peers:
        best_copy(peer, f).start()
    returned[f] = best[lax.div(f, group)]
    pick = lax.broadcasted_iota(jnp.int32, (LANES, rows), 0) == rank + lax.rem(f * slot, LANES)
    pick = jnp.where(pick, 1.0, 0.0).astype(jnp.bfloat16)
    mine = lax.broadcasted_iota(jnp.int32, (F * 8, rows), 0) == label_row * 8
    for k in range(1, F):
        best_copy(fine_peer(k), fine_peer(k)).wait_recv()
    values = returned[...].reshape(F * 8, LANES)
    high, rest = values.astype(jnp.bfloat16), None
    rest = values - high.astype(jnp.float32)
    middle, low = split_two(rest)
    found = dot(high, pick) + (dot(middle, pick) + dot(low, pick))
    out[...] = jnp.sum(jnp.where(mine, found, 0.0), axis=0, keepdims=True)

    core_copy.wait_send()
    core_gather(core).wait_send()
    for k in range(1, C):
        coarse_copy(coarse_peer(k), c).wait_send()
        coarse_gather(coarse_peer(k), c).wait_send()
    for k in range(1, Z):
        z_copy(z_peer(k), z).wait_send()
        z_gather(z_peer(k), z).wait_send()
    for k in range(1, F):
        row_copy(fine_peer(k), f).wait_send()
        count_copy(fine_peer(k), f).wait_send()
        best_copy(fine_peer(k), f).wait_send()


def per_device(embeddings, labels):
    rows, width = embeddings.shape
    F = lax.axis_size("fine")
    C = lax.axis_size("coarse")
    Z = F // 2
    slot = 2 * rows // F
    slots = F * slot
    blocks = width // LANES
    unit_rows = 8 * C * F
    stack_rows = -(-(blocks * (blocks + 1) // 2 * LANES) // unit_rows) * unit_rows
    half_rows = stack_rows // 2
    part_rows = half_rows // C
    piece_rows = part_rows // Z
    f32, bf16 = jnp.float32, jnp.bfloat16
    dma = pltpu.SemaphoreType.DMA
    best = pl.pallas_call(
        functools.partial(kernel, C, F, slot, stack_rows, rows * F * C),
        out_shape=jax.ShapeDtypeStruct((1, rows), f32),
        in_specs=[pl.BlockSpec(memory_space=pl.ANY)] * 2,
        out_specs=pl.BlockSpec(memory_space=pltpu.VMEM),
        scratch_shapes=[
            pltpu.VMEM((rows, width), bf16),
            pltpu.VMEM((1, rows), jnp.int32),
            pltpu.VMEM((stack_rows, LANES), f32),
            pltpu.VMEM((half_rows, LANES), f32),
            pltpu.VMEM((half_rows, LANES), f32),
            pltpu.VMEM((C, part_rows, LANES), f32),
            pltpu.VMEM((part_rows, LANES), f32),
            pltpu.VMEM((Z, piece_rows, LANES), f32),
            pltpu.VMEM((stack_rows, LANES), f32),
            pltpu.VMEM((slots, width), bf16),
            pltpu.VMEM((slots, width), bf16),
            pltpu.VMEM((F, 8, LANES), f32),
            pltpu.VMEM((F, 8, LANES), f32),
            pltpu.VMEM((width, width), f32),
            pltpu.VMEM((width, width), bf16),
            pltpu.VMEM((slots, width), bf16),
            pltpu.VMEM((slots // LANES, 8, LANES), f32),
            pltpu.VMEM((F, 8, LANES), f32),
            dma, dma,
            dma, dma, dma((C,)), dma((C,)), dma((Z,)), dma((Z,)),
            dma((Z,)), dma((Z,)), dma((C,)), dma((C,)), dma, dma,
            dma((F,)), dma((F,)), dma((F,)), dma((F,)), dma((F,)), dma((F,)),
        ],
        compiler_params=pltpu.CompilerParams(
            collective_id=0, has_side_effects=True, vmem_limit_bytes=60 * 1024 * 1024
        ),
    )(embeddings, labels.reshape(1, rows))
    return best.reshape(rows)


def solution(mesh):
    in_specs = (P(("coarse", "fine"), None), P(("coarse", "fine"), None))
    out_specs = P(("coarse", "fine"))
    return jax.shard_map(
        per_device, mesh=mesh, in_specs=in_specs, out_specs=out_specs, check_vma=False
    )
```

```python
import functools

import jax
import jax.numpy as jnp
from jax import lax
from jax.experimental import pallas as pl
from jax.experimental.pallas import tpu as pltpu
from jax.sharding import PartitionSpec as P

EPS = 1e-06
RIDGE = 0.001
LANES = 128
LOW = -3.0e38
MESH = pl.DeviceIdType.MESH


def dot(left, right):
    return jnp.dot(left, right, preferred_element_type=jnp.float32)


def split_two(value):
    high = value.astype(jnp.bfloat16)
    return high, (value - high.astype(jnp.float32)).astype(jnp.bfloat16)


def remote(src, dst, send_sem, recv_sem, device):
    return pltpu.make_async_remote_copy(
        src_ref=src, dst_ref=dst, send_sem=send_sem, recv_sem=recv_sem,
        device_id=device, device_id_type=MESH,
    )


def rows_at(ref, start, size):
    return ref.at[pl.ds(pl.multiple_of(start, 8), size)]


def kernel(
    C, F, slot, stack_rows, row_total,
    emb_hbm, labels_hbm, out,
    emb, labels, acc, half_in, half, coarse_in, part, z_in, total,
    outgoing, received, counts_out, counts_in, full, whiten, unit, best, returned,
    emb_sem, labels_sem,    core_s, core_r, coarse_s, coarse_r, z_s, z_r, gz_s, gz_r, gc_s, gc_r, gk_s, gk_r,
    a_s, a_r, n_s, n_r, b_s, b_r,
):
    emb_copy = pltpu.make_async_copy(emb_hbm, emb, emb_sem)
    labels_copy = pltpu.make_async_copy(labels_hbm, labels, labels_sem)
    emb_copy.start()
    labels_copy.start()
    rows, width = emb.shape
    blocks = width // LANES
    pairs = [(i, j) for i in range(blocks) for j in range(i, blocks)]
    Z = F // 2
    slots = F * slot
    c = lax.axis_index("coarse")
    f = lax.axis_index("fine")
    core = lax.rem(f, 2)
    z = lax.div(f, 2)
    sibling = (c, f + 1 - 2 * core)

    def fine_peer(k):
        return lax.rem(f + k, F)

    def coarse_peer(k):
        return lax.rem(c + k, C)

    def z_peer(k):
        return lax.rem(z + k, Z)

    def z_other(k, flip):
        return 2 * z_peer(k) + (1 - core if flip else core)

    steps = sorted(range(1, Z), key=lambda k: min(k, Z - k))
    far = [z_other(k, flip) for k in steps for flip in (False, True)]
    early, middle = len(far) // 3, len(far) // 3 + len(far) // 6
    lots = [far[:early] + [z_other(0, True)], far[early:middle], far[middle + 1:] + [far[middle]]]
    peers = lots[0] + lots[1] + lots[2]

    barrier = pltpu.get_barrier_semaphore()
    for k in range(1, F):
        pl.semaphore_signal(barrier, inc=1, device_id=(c, fine_peer(k)), device_id_type=MESH)
    for k in range(1, C):
        pl.semaphore_signal(barrier, inc=1, device_id=(coarse_peer(k), f), device_id_type=MESH)

    emb_copy.wait()
    used = len(pairs) * LANES
    if stack_rows > used:
        acc[used:, :] = jnp.zeros((stack_rows - used, LANES), jnp.float32)
    place = 0
    for i in range(blocks):
        strip = lax.dot_general(
            emb[:, i * LANES:(i + 1) * LANES], emb[:, i * LANES:],
            (((0,), (0,)), ((), ())), preferred_element_type=jnp.float32,
        )
        for j in range(blocks - i):
            acc[place * LANES:(place + 1) * LANES, :] = strip[:, j * LANES:(j + 1) * LANES]
            place += 1
    pl.semaphore_wait(barrier, F + C - 2)

    half_rows = stack_rows // 2
    part_rows = half_rows // C
    piece_rows = part_rows // Z

    core_copy = remote(
        rows_at(acc, (1 - core) * half_rows, half_rows), half_in, core_s, core_r, sibling
    )
    core_copy.start()

    labels_copy.wait()
    label_row = labels[...]
    onehot = lax.broadcasted_iota(jnp.int32, (F, rows), 0) == label_row
    before = (
        lax.broadcasted_iota(jnp.int32, (rows, rows), 0)
        < lax.broadcasted_iota(jnp.int32, (rows, rows), 1)
    )
    flags = jnp.where(onehot, 1.0, 0.0)
    rank_all = dot(flags.astype(jnp.bfloat16), jnp.where(before, 1.0, 0.0).astype(jnp.bfloat16))
    rank = jnp.sum(jnp.where(onehot, rank_all, 0.0), axis=0, keepdims=True).astype(jnp.int32)
    amounts = jnp.sum(flags, axis=1, keepdims=True)
    for label in range(F):
        counts_out[label] = jnp.broadcast_to(amounts[label:label + 1, :], (8, LANES))
    slot_of = label_row * slot + rank
    def slot_rows(ref, which):
        return ref.at[pl.ds(pl.multiple_of(which * slot, 16), slot)]

    def row_copy(to, source):
        return remote(
            slot_rows(outgoing, to), slot_rows(received, source), a_s.at[to], a_r.at[source], (c, to)
        )

    def count_copy(to, source):
        return remote(counts_out.at[to], counts_in.at[source], n_s.at[to], n_r.at[source], (c, to))

    def compact(devices):
        places = lax.broadcasted_iota(jnp.int32, (slot, rows), 0)
        picks = [
            jnp.where(places + to * slot == slot_of, 1.0, 0.0).astype(jnp.bfloat16) for to in devices
        ]
        picked = dot(jnp.concatenate(picks, axis=0), emb[...]).astype(jnp.bfloat16)
        for n, to in enumerate(devices):
            slot_rows(outgoing, to)[...] = picked[n * slot:(n + 1) * slot, :]

    compact(lots[0])

    core_copy.wait_recv()
    half[...] = rows_at(acc, core * half_rows, half_rows)[...] + half_in[...]

    def coarse_copy(to, source):
        return remote(
            rows_at(half, to * part_rows, part_rows), coarse_in.at[source],
            coarse_s.at[to], coarse_r.at[source], (to, f),
        )

    for k in range(1, C):
        coarse_copy(coarse_peer(k), c).start()
    for peer in lots[0]:
        row_copy(peer, f).start()
    for peer in peers:
        count_copy(peer, f).start()
    compact(lots[1] + lots[2] + [f])
    slot_rows(received, f)[...] = slot_rows(outgoing, f)[...]
    counts_in[f] = counts_out[f]
    value = rows_at(half, c * part_rows, part_rows)[...]
    for k in range(1, C):
        coarse_copy(coarse_peer(k), coarse_peer(k)).wait_recv()
        value = value + coarse_in[coarse_peer(k)]
    part[...] = value

    def z_copy(to, source):
        return remote(
            rows_at(part, to * piece_rows, piece_rows), z_in.at[source],
            z_s.at[to], z_r.at[source], (c, 2 * to + core),
        )

    for k in range(1, Z):
        z_copy(z_peer(k), z).start()
    for peer in lots[1]:
        row_copy(peer, f).start()
    value = rows_at(part, z * piece_rows, piece_rows)[...]
    for k in range(1, Z):
        z_copy(z_peer(k), z_peer(k)).wait_recv()
        value = value + z_in[z_peer(k)]

    def piece_start(coarse_id, z_id):
        return core * half_rows + coarse_id * part_rows + z_id * piece_rows

    rows_at(total, piece_start(c, z), piece_rows)[...] = value

    def z_gather(to, source):
        piece = rows_at(total, piece_start(c, source), piece_rows)
        return remote(piece, piece, gz_s.at[to], gz_r.at[source], (c, 2 * to + core))

    def coarse_gather(to, source):
        piece = rows_at(total, piece_start(source, 0), part_rows)
        return remote(piece, piece, gc_s.at[to], gc_r.at[source], (to, f))

    def core_gather(source):
        piece = rows_at(total, source * half_rows, half_rows)
        return remote(piece, piece, gk_s, gk_r, sibling)

    for k in range(1, Z):
        z_gather(z_peer(k), z).start()
    for peer in lots[2]:
        row_copy(peer, f).start()
    for k in range(1, Z):
        z_gather(z_peer(k), z_peer(k)).wait_recv()
    for k in range(1, C):
        coarse_gather(coarse_peer(k), c).start()
    for k in range(1, C):
        coarse_gather(coarse_peer(k), coarse_peer(k)).wait_recv()
    core_gather(core).start()

    for k in range(1, F):
        count_copy(fine_peer(k), fine_peer(k)).wait_recv()

    core_gather(1 - core).wait_recv()
    for place, (i, j) in enumerate(pairs):
        block = total[place * LANES:(place + 1) * LANES, :] * (1.0 / row_total)
        if i == j:
            diagonal = (
                lax.broadcasted_iota(jnp.int32, (LANES, LANES), 0)
                == lax.broadcasted_iota(jnp.int32, (LANES, LANES), 1)
            )
            block = block + jnp.where(diagonal, RIDGE, 0.0)
        else:
            full[j * LANES:(j + 1) * LANES, i * LANES:(i + 1) * LANES] = block.T
        full[i * LANES:(i + 1) * LANES, j * LANES:(j + 1) * LANES] = block
    second = full[...]
    norm_scale = jnp.max(jnp.sum(jnp.abs(second), axis=0, keepdims=True), axis=1, keepdims=True)
    root = second * (1.0 / norm_scale)
    identity = jnp.where(
        lax.broadcasted_iota(jnp.int32, (width, width), 0)
        == lax.broadcasted_iota(jnp.int32, (width, width), 1),
        2.25, 0.0,
    )
    root_b = root.astype(jnp.bfloat16)
    square = dot(root_b, root_b)
    outer = (0.0625 * square - 0.5625 * root).astype(jnp.bfloat16)
    inverse = identity - 2.4375 * root + 1.6875 * square + dot(square.astype(jnp.bfloat16), outer)
    whiten[...] = (inverse * (1.0 / jnp.sqrt(norm_scale))).astype(jnp.bfloat16)

    group = LANES // slot
    if group == 1:
        order = [f] + peers
    else:
        order = [lax.rem(lax.div(f, group) + n, F // group) for n in range(F // group)]
        for peer in peers:
            row_copy(peer, peer).wait_recv()
    rank_here = lax.broadcasted_iota(jnp.int32, (slot, LANES), 0).astype(jnp.float32)
    diagonal = (
        lax.broadcasted_iota(jnp.int32, (LANES, LANES), 0)
        == lax.broadcasted_iota(jnp.int32, (LANES, LANES), 1)
    )

    def highest(tile):
        return jnp.max(tile.reshape(LANES // 8, 8, LANES), axis=0)

    tops, biases = [], []
    for n, block in enumerate(order):
        if group == 1 and n > 0:
            row_copy(block, block).wait_recv()
        white = dot(rows_at(received, block * LANES, LANES)[...], whiten[...])
        meansq = jnp.mean(white * white, axis=-1, keepdims=True)
        here = (white * lax.rsqrt(width * (meansq + EPS))).astype(jnp.bfloat16)
        unit[n * LANES:(n + 1) * LANES, :] = here
        bias = [
            jnp.where(rank_here < counts_in[block * group + m][0:1, :], 0.0, LOW) for m in range(group)
        ]
        bias = bias[0] if group == 1 else jnp.concatenate(bias, axis=0)
        so_far = unit[0:(n + 1) * LANES, :]
        down = lax.dot_general(here, so_far, (((1,), (1,)), ((), ())), preferred_element_type=jnp.float32)
        for t in range(n):
            tops[t] = jnp.maximum(tops[t], highest(down[:, t * LANES:(t + 1) * LANES] + bias))
        top = highest(jnp.where(diagonal, LOW, down[:, n * LANES:] + bias))
        if n > 0:
            across = lax.dot_general(
                unit[0:n * LANES, :], here, (((1,), (1,)), ((), ())), preferred_element_type=jnp.float32
            )
            for t in range(n):
                top = jnp.maximum(top, highest(across[t * LANES:(t + 1) * LANES, :] + biases[t]))
        tops.append(jnp.maximum(top, -1.0))
        biases.append(bias)
    for n, block in enumerate(order):
        best[block] = jnp.broadcast_to(jnp.max(tops[n], axis=0, keepdims=True), (8, LANES))

    def best_copy(to, source):
        return remote(
            best.at[lax.div(to, group)], returned.at[source], b_s.at[to], b_r.at[source], (c, to)
        )

    for peer in peers:
        best_copy(peer, f).start()
    returned[f] = best[lax.div(f, group)]
    pick = lax.broadcasted_iota(jnp.int32, (LANES, rows), 0) == rank + lax.rem(f * slot, LANES)
    pick = jnp.where(pick, 1.0, 0.0).astype(jnp.bfloat16)
    mine = lax.broadcasted_iota(jnp.int32, (F * 8, rows), 0) == label_row * 8
    for k in range(1, F):
        best_copy(fine_peer(k), fine_peer(k)).wait_recv()
    values = returned[...].reshape(F * 8, LANES)
    high, rest = values.astype(jnp.bfloat16), None
    rest = values - high.astype(jnp.float32)
    middle, low = split_two(rest)
    found = dot(high, pick) + (dot(middle, pick) + dot(low, pick))
    out[...] = jnp.sum(jnp.where(mine, found, 0.0), axis=0, keepdims=True)

    core_copy.wait_send()
    core_gather(core).wait_send()
    for k in range(1, C):
        coarse_copy(coarse_peer(k), c).wait_send()
        coarse_gather(coarse_peer(k), c).wait_send()
    for k in range(1, Z):
        z_copy(z_peer(k), z).wait_send()
        z_gather(z_peer(k), z).wait_send()
    for k in range(1, F):
        row_copy(fine_peer(k), f).wait_send()
        count_copy(fine_peer(k), f).wait_send()
        best_copy(fine_peer(k), f).wait_send()


def per_device(embeddings, labels):
    rows, width = embeddings.shape
    F = lax.axis_size("fine")
    C = lax.axis_size("coarse")
    Z = F // 2
    slot = 2 * rows // F
    slots = F * slot
    blocks = width // LANES
    unit_rows = 8 * C * F
    stack_rows = -(-(blocks * (blocks + 1) // 2 * LANES) // unit_rows) * unit_rows
    half_rows = stack_rows // 2
    part_rows = half_rows // C
    piece_rows = part_rows // Z
    f32, bf16 = jnp.float32, jnp.bfloat16
    dma = pltpu.SemaphoreType.DMA
    best = pl.pallas_call(
        functools.partial(kernel, C, F, slot, stack_rows, rows * F * C),
        out_shape=jax.ShapeDtypeStruct((1, rows), f32),
        in_specs=[pl.BlockSpec(memory_space=pl.ANY)] * 2,
        out_specs=pl.BlockSpec(memory_space=pltpu.VMEM),
        scratch_shapes=[
            pltpu.VMEM((rows, width), bf16),
            pltpu.VMEM((1, rows), jnp.int32),
            pltpu.VMEM((stack_rows, LANES), f32),
            pltpu.VMEM((half_rows, LANES), f32),
            pltpu.VMEM((half_rows, LANES), f32),
            pltpu.VMEM((C, part_rows, LANES), f32),
            pltpu.VMEM((part_rows, LANES), f32),
            pltpu.VMEM((Z, piece_rows, LANES), f32),
            pltpu.VMEM((stack_rows, LANES), f32),
            pltpu.VMEM((slots, width), bf16),
            pltpu.VMEM((slots, width), bf16),
            pltpu.VMEM((F, 8, LANES), f32),
            pltpu.VMEM((F, 8, LANES), f32),
            pltpu.VMEM((width, width), f32),
            pltpu.VMEM((width, width), bf16),
            pltpu.VMEM((slots, width), bf16),
            pltpu.VMEM((slots // LANES, 8, LANES), f32),
            pltpu.VMEM((F, 8, LANES), f32),
            dma, dma,
            dma, dma, dma((C,)), dma((C,)), dma((Z,)), dma((Z,)),
            dma((Z,)), dma((Z,)), dma((C,)), dma((C,)), dma, dma,
            dma((F,)), dma((F,)), dma((F,)), dma((F,)), dma((F,)), dma((F,)),
        ],
        compiler_params=pltpu.CompilerParams(
            collective_id=0, has_side_effects=True, vmem_limit_bytes=(64 * 1024 - 256) * 1024
        ),
    )(embeddings, labels.reshape(1, rows))
    return best.reshape(rows)


def solution(mesh):
    in_specs = (P(("coarse", "fine"), None), P(("coarse", "fine"), None))
    out_specs = P(("coarse", "fine"))
    return jax.shard_map(
        per_device, mesh=mesh, in_specs=in_specs, out_specs=out_specs, check_vma=False
    )
```

```python
import functools

import jax
import jax.numpy as jnp
from jax import lax
from jax.experimental import pallas as pl
from jax.experimental.pallas import tpu as pltpu
from jax.sharding import PartitionSpec as P

EPS = 1e-06
RIDGE = 0.001
LANES = 128
LOW = -3.0e38
MESH = pl.DeviceIdType.MESH


def dot(left, right):
    return jnp.dot(left, right, preferred_element_type=jnp.float32)


def split_two(value):
    high = value.astype(jnp.bfloat16)
    return high, (value - high.astype(jnp.float32)).astype(jnp.bfloat16)


def remote(src, dst, send_sem, recv_sem, device):
    return pltpu.make_async_remote_copy(
        src_ref=src, dst_ref=dst, send_sem=send_sem, recv_sem=recv_sem,
        device_id=device, device_id_type=MESH,
    )


def rows_at(ref, start, size):
    return ref.at[pl.ds(pl.multiple_of(start, 8), size)]


def kernel(
    C, F, slot, stack_rows, row_total,
    emb_hbm, labels_hbm, out,
    emb, labels, acc, half_in, half, coarse_in, part, z_in, total,
    outgoing, received, counts_out, counts_in, full, whiten, unit, best, returned,
    emb_sem, labels_sem,    core_s, core_r, coarse_s, coarse_r, z_s, z_r, gz_s, gz_r, gc_s, gc_r, gk_s, gk_r,
    a_s, a_r, n_s, n_r, b_s, b_r,
):
    emb_copy = pltpu.make_async_copy(emb_hbm, emb, emb_sem)
    labels_copy = pltpu.make_async_copy(labels_hbm, labels, labels_sem)
    emb_copy.start()
    labels_copy.start()
    rows, width = emb.shape
    blocks = width // LANES
    pairs = [(i, j) for i in range(blocks) for j in range(i, blocks)]
    Z = F // 2
    slots = F * slot
    c = lax.axis_index("coarse")
    f = lax.axis_index("fine")
    core = lax.rem(f, 2)
    z = lax.div(f, 2)
    sibling = (c, f + 1 - 2 * core)

    def fine_peer(k):
        return lax.rem(f + k, F)

    def coarse_peer(k):
        return lax.rem(c + k, C)

    def z_peer(k):
        return lax.rem(z + k, Z)

    def z_other(k, flip):
        return 2 * z_peer(k) + (1 - core if flip else core)

    steps = sorted(range(1, Z), key=lambda k: min(k, Z - k))
    far = [z_other(k, flip) for k in steps for flip in (False, True)]
    early, middle = len(far) // 3, len(far) // 3 + len(far) // 6
    lots = [far[:early] + [z_other(0, True)], far[early:middle], far[middle + 1:] + [far[middle]]]
    peers = lots[0] + lots[1] + lots[2]

    barrier = pltpu.get_barrier_semaphore()
    for k in range(1, F):
        pl.semaphore_signal(barrier, inc=1, device_id=(c, fine_peer(k)), device_id_type=MESH)
    for k in range(1, C):
        pl.semaphore_signal(barrier, inc=1, device_id=(coarse_peer(k), f), device_id_type=MESH)

    emb_copy.wait()
    used = len(pairs) * LANES
    if stack_rows > used:
        acc[used:, :] = jnp.zeros((stack_rows - used, LANES), jnp.float32)
    place = 0
    for i in range(blocks):
        strip = lax.dot_general(
            emb[:, i * LANES:(i + 1) * LANES], emb[:, i * LANES:],
            (((0,), (0,)), ((), ())), preferred_element_type=jnp.float32,
        )
        for j in range(blocks - i):
            acc[place * LANES:(place + 1) * LANES, :] = strip[:, j * LANES:(j + 1) * LANES]
            place += 1
    pl.semaphore_wait(barrier, F + C - 2)

    half_rows = stack_rows // 2
    part_rows = half_rows // C
    piece_rows = part_rows // Z

    core_copy = remote(
        rows_at(acc, (1 - core) * half_rows, half_rows), half_in, core_s, core_r, sibling
    )
    core_copy.start()

    labels_copy.wait()
    label_row = labels[...]
    onehot = lax.broadcasted_iota(jnp.int32, (F, rows), 0) == label_row
    before = (
        lax.broadcasted_iota(jnp.int32, (rows, rows), 0)
        < lax.broadcasted_iota(jnp.int32, (rows, rows), 1)
    )
    flags = jnp.where(onehot, 1.0, 0.0)
    rank_all = dot(flags.astype(jnp.bfloat16), jnp.where(before, 1.0, 0.0).astype(jnp.bfloat16))
    rank = jnp.sum(jnp.where(onehot, rank_all, 0.0), axis=0, keepdims=True).astype(jnp.int32)
    amounts = jnp.sum(flags, axis=1, keepdims=True)
    for label in range(F):
        counts_out[label] = jnp.broadcast_to(amounts[label:label + 1, :], (8, LANES))
    slot_of = label_row * slot + rank
    def slot_rows(ref, which):
        return ref.at[pl.ds(pl.multiple_of(which * slot, 16), slot)]

    def row_copy(to, source):
        return remote(
            slot_rows(outgoing, to), slot_rows(received, source), a_s.at[to], a_r.at[source], (c, to)
        )

    def count_copy(to, source):
        return remote(counts_out.at[to], counts_in.at[source], n_s.at[to], n_r.at[source], (c, to))

    def compact(devices):
        places = lax.broadcasted_iota(jnp.int32, (slot, rows), 0)
        picks = [
            jnp.where(places + to * slot == slot_of, 1.0, 0.0).astype(jnp.bfloat16) for to in devices
        ]
        picked = dot(jnp.concatenate(picks, axis=0), emb[...]).astype(jnp.bfloat16)
        for n, to in enumerate(devices):
            slot_rows(outgoing, to)[...] = picked[n * slot:(n + 1) * slot, :]

    compact(lots[0])

    core_copy.wait_recv()
    half[...] = rows_at(acc, core * half_rows, half_rows)[...] + half_in[...]

    def coarse_copy(to, source):
        return remote(
            rows_at(half, to * part_rows, part_rows), coarse_in.at[source],
            coarse_s.at[to], coarse_r.at[source], (to, f),
        )

    for k in range(1, C):
        coarse_copy(coarse_peer(k), c).start()
    for peer in lots[0]:
        row_copy(peer, f).start()
    for peer in peers:
        count_copy(peer, f).start()
    compact(lots[1] + lots[2] + [f])
    slot_rows(received, f)[...] = slot_rows(outgoing, f)[...]
    counts_in[f] = counts_out[f]
    value = rows_at(half, c * part_rows, part_rows)[...]
    for k in range(1, C):
        coarse_copy(coarse_peer(k), coarse_peer(k)).wait_recv()
        value = value + coarse_in[coarse_peer(k)]
    part[...] = value

    def z_copy(to, source):
        return remote(
            rows_at(part, to * piece_rows, piece_rows), z_in.at[source],
            z_s.at[to], z_r.at[source], (c, 2 * to + core),
        )

    for k in range(1, Z):
        z_copy(z_peer(k), z).start()
    for peer in lots[1]:
        row_copy(peer, f).start()
    value = rows_at(part, z * piece_rows, piece_rows)[...]
    for k in range(1, Z):
        z_copy(z_peer(k), z_peer(k)).wait_recv()
        value = value + z_in[z_peer(k)]

    def piece_start(coarse_id, z_id):
        return core * half_rows + coarse_id * part_rows + z_id * piece_rows

    rows_at(total, piece_start(c, z), piece_rows)[...] = value

    def z_gather(to, source):
        piece = rows_at(total, piece_start(c, source), piece_rows)
        return remote(piece, piece, gz_s.at[to], gz_r.at[source], (c, 2 * to + core))

    def coarse_gather(to, source):
        piece = rows_at(total, piece_start(source, 0), part_rows)
        return remote(piece, piece, gc_s.at[to], gc_r.at[source], (to, f))

    def core_gather(source):
        piece = rows_at(total, source * half_rows, half_rows)
        return remote(piece, piece, gk_s, gk_r, sibling)

    for k in range(1, Z):
        z_gather(z_peer(k), z).start()
    for peer in lots[2]:
        row_copy(peer, f).start()
    for k in range(1, Z):
        z_gather(z_peer(k), z_peer(k)).wait_recv()
    for k in range(1, C):
        coarse_gather(coarse_peer(k), c).start()
    for k in range(1, C):
        coarse_gather(coarse_peer(k), coarse_peer(k)).wait_recv()
    core_gather(core).start()

    for k in range(1, F):
        count_copy(fine_peer(k), fine_peer(k)).wait_recv()

    core_gather(1 - core).wait_recv()
    for place, (i, j) in enumerate(pairs):
        block = total[place * LANES:(place + 1) * LANES, :] * (1.0 / row_total)
        if i == j:
            diagonal = (
                lax.broadcasted_iota(jnp.int32, (LANES, LANES), 0)
                == lax.broadcasted_iota(jnp.int32, (LANES, LANES), 1)
            )
            block = block + jnp.where(diagonal, RIDGE, 0.0)
        else:
            full[j * LANES:(j + 1) * LANES, i * LANES:(i + 1) * LANES] = block.T
        full[i * LANES:(i + 1) * LANES, j * LANES:(j + 1) * LANES] = block
    second = full[...]
    norm_scale = jnp.max(jnp.sum(jnp.abs(second), axis=0, keepdims=True), axis=1, keepdims=True)
    root = second * (1.0 / norm_scale)
    identity = jnp.where(
        lax.broadcasted_iota(jnp.int32, (width, width), 0)
        == lax.broadcasted_iota(jnp.int32, (width, width), 1),
        2.25, 0.0,
    )
    root_b = root.astype(jnp.bfloat16)
    square = dot(root_b, root_b)
    outer = (0.0625 * square - 0.5625 * root).astype(jnp.bfloat16)
    inverse = identity - 2.4375 * root + 1.6875 * square + dot(square.astype(jnp.bfloat16), outer)
    whiten[...] = (inverse * (1.0 / jnp.sqrt(norm_scale))).astype(jnp.bfloat16)

    group = LANES // slot
    if group == 1:
        batches = [[f] + lots[0] + lots[1], lots[2]]
    else:
        batches = [[lax.rem(lax.div(f, group) + n, F // group) for n in range(F // group)]]
        for peer in peers:
            row_copy(peer, peer).wait_recv()
    order = sum(batches, [])
    rank_here = lax.broadcasted_iota(jnp.int32, (slot, LANES), 0).astype(jnp.float32)
    diagonal = (
        lax.broadcasted_iota(jnp.int32, (LANES, LANES), 0)
        == lax.broadcasted_iota(jnp.int32, (LANES, LANES), 1)
    )

    def highest(tile):
        return jnp.max(tile.reshape(LANES // 8, 8, LANES), axis=0)

    tops, biases, done = [], [], 0
    for batch in batches:
        if group == 1:
            for block in batch:
                if block is not f:
                    row_copy(block, block).wait_recv()
        arrived = [rows_at(received, block * LANES, LANES)[...] for block in batch]
        white = dot(jnp.concatenate(arrived, axis=0), whiten[...])
        meansq = jnp.mean(white * white, axis=-1, keepdims=True)
        here = (white * lax.rsqrt(width * (meansq + EPS))).astype(jnp.bfloat16)
        end = done + len(batch)
        unit[done * LANES:end * LANES, :] = here
        for block in batch:
            bias = [
                jnp.where(rank_here < counts_in[block * group + m][0:1, :], 0.0, LOW) for m in range(group)
            ]
            biases.append(bias[0] if group == 1 else jnp.concatenate(bias, axis=0))
            tops.append(jnp.full((8, LANES), -1.0, jnp.float32))
        down = lax.dot_general(
            here, unit[0:end * LANES, :], (((1,), (1,)), ((), ())), preferred_element_type=jnp.float32
        )
        for q in range(done, end):
            for t in range(end):
                tile = down[(q - done) * LANES:(q - done + 1) * LANES, t * LANES:(t + 1) * LANES] + biases[q]
                if t == q:
                    tile = jnp.where(diagonal, LOW, tile)
                tops[t] = jnp.maximum(tops[t], highest(tile))
        if done > 0:
            across = lax.dot_general(
                unit[0:done * LANES, :], here, (((1,), (1,)), ((), ())), preferred_element_type=jnp.float32
            )
            for q in range(done):
                for t in range(done, end):
                    tile = across[q * LANES:(q + 1) * LANES, (t - done) * LANES:(t - done + 1) * LANES]
                    tops[t] = jnp.maximum(tops[t], highest(tile + biases[q]))
        done = end
    for n, block in enumerate(order):
        best[block] = jnp.broadcast_to(jnp.max(tops[n], axis=0, keepdims=True), (8, LANES))

    def best_copy(to, source):
        return remote(
            best.at[lax.div(to, group)], returned.at[source], b_s.at[to], b_r.at[source], (c, to)
        )

    for peer in peers:
        best_copy(peer, f).start()
    returned[f] = best[lax.div(f, group)]
    pick = lax.broadcasted_iota(jnp.int32, (LANES, rows), 0) == rank + lax.rem(f * slot, LANES)
    pick = jnp.where(pick, 1.0, 0.0).astype(jnp.bfloat16)
    mine = lax.broadcasted_iota(jnp.int32, (F * 8, rows), 0) == label_row * 8
    for k in range(1, F):
        best_copy(fine_peer(k), fine_peer(k)).wait_recv()
    values = returned[...].reshape(F * 8, LANES)
    high, rest = values.astype(jnp.bfloat16), None
    rest = values - high.astype(jnp.float32)
    middle, low = split_two(rest)
    found = dot(high, pick) + (dot(middle, pick) + dot(low, pick))
    out[...] = jnp.sum(jnp.where(mine, found, 0.0), axis=0, keepdims=True)

    core_copy.wait_send()
    core_gather(core).wait_send()
    for k in range(1, C):
        coarse_copy(coarse_peer(k), c).wait_send()
        coarse_gather(coarse_peer(k), c).wait_send()
    for k in range(1, Z):
        z_copy(z_peer(k), z).wait_send()
        z_gather(z_peer(k), z).wait_send()
    for k in range(1, F):
        row_copy(fine_peer(k), f).wait_send()
        count_copy(fine_peer(k), f).wait_send()
        best_copy(fine_peer(k), f).wait_send()


def per_device(embeddings, labels):
    rows, width = embeddings.shape
    F = lax.axis_size("fine")
    C = lax.axis_size("coarse")
    Z = F // 2
    slot = 2 * rows // F
    slots = F * slot
    blocks = width // LANES
    unit_rows = 8 * C * F
    stack_rows = -(-(blocks * (blocks + 1) // 2 * LANES) // unit_rows) * unit_rows
    half_rows = stack_rows // 2
    part_rows = half_rows // C
    piece_rows = part_rows // Z
    f32, bf16 = jnp.float32, jnp.bfloat16
    dma = pltpu.SemaphoreType.DMA
    best = pl.pallas_call(
        functools.partial(kernel, C, F, slot, stack_rows, rows * F * C),
        out_shape=jax.ShapeDtypeStruct((1, rows), f32),
        in_specs=[pl.BlockSpec(memory_space=pl.ANY)] * 2,
        out_specs=pl.BlockSpec(memory_space=pltpu.VMEM),
        scratch_shapes=[
            pltpu.VMEM((rows, width), bf16),
            pltpu.VMEM((1, rows), jnp.int32),
            pltpu.VMEM((stack_rows, LANES), f32),
            pltpu.VMEM((half_rows, LANES), f32),
            pltpu.VMEM((half_rows, LANES), f32),
            pltpu.VMEM((C, part_rows, LANES), f32),
            pltpu.VMEM((part_rows, LANES), f32),
            pltpu.VMEM((Z, piece_rows, LANES), f32),
            pltpu.VMEM((stack_rows, LANES), f32),
            pltpu.VMEM((slots, width), bf16),
            pltpu.VMEM((slots, width), bf16),
            pltpu.VMEM((F, 8, LANES), f32),
            pltpu.VMEM((F, 8, LANES), f32),
            pltpu.VMEM((width, width), f32),
            pltpu.VMEM((width, width), bf16),
            pltpu.VMEM((slots, width), bf16),
            pltpu.VMEM((slots // LANES, 8, LANES), f32),
            pltpu.VMEM((F, 8, LANES), f32),
            dma, dma,
            dma, dma, dma((C,)), dma((C,)), dma((Z,)), dma((Z,)),
            dma((Z,)), dma((Z,)), dma((C,)), dma((C,)), dma, dma,
            dma((F,)), dma((F,)), dma((F,)), dma((F,)), dma((F,)), dma((F,)),
        ],
        compiler_params=pltpu.CompilerParams(
            collective_id=0, has_side_effects=True, vmem_limit_bytes=(64 * 1024 - 256) * 1024
        ),
    )(embeddings, labels.reshape(1, rows))
    return best.reshape(rows)


def solution(mesh):
    in_specs = (P(("coarse", "fine"), None), P(("coarse", "fine"), None))
    out_specs = P(("coarse", "fine"))
    return jax.shard_map(
        per_device, mesh=mesh, in_specs=in_specs, out_specs=out_specs, check_vma=False
    )
```

```python
import functools

import jax
import jax.numpy as jnp
from jax import lax
from jax.experimental import pallas as pl
from jax.experimental.pallas import tpu as pltpu
from jax.sharding import PartitionSpec as P

EPS = 1e-06
RIDGE = 0.001
LANES = 128
LOW = -3.0e38
MESH = pl.DeviceIdType.MESH


def dot(left, right):
    return jnp.dot(left, right, preferred_element_type=jnp.float32)


def split_two(value):
    high = value.astype(jnp.bfloat16)
    return high, (value - high.astype(jnp.float32)).astype(jnp.bfloat16)


def remote(src, dst, send_sem, recv_sem, device):
    return pltpu.make_async_remote_copy(
        src_ref=src, dst_ref=dst, send_sem=send_sem, recv_sem=recv_sem,
        device_id=device, device_id_type=MESH,
    )


def rows_at(ref, start, size):
    return ref.at[pl.ds(pl.multiple_of(start, 8), size)]


def kernel(
    C, F, slot, stack_rows, row_total,
    emb_hbm, labels_hbm, out,
    emb, labels, acc, half_in, half, coarse_in, part, z_in, total,
    outgoing, received, counts_out, counts_in, full, whiten, unit, best, returned,
    emb_sem, labels_sem,    core_s, core_r, coarse_s, coarse_r, z_s, z_r, gz_s, gz_r, gc_s, gc_r, gk_s, gk_r,
    a_s, a_r, n_s, n_r, b_s, b_r,
):
    emb_copy = pltpu.make_async_copy(emb_hbm, emb, emb_sem)
    labels_copy = pltpu.make_async_copy(labels_hbm, labels, labels_sem)
    emb_copy.start()
    labels_copy.start()
    rows, width = emb.shape
    blocks = width // LANES
    pairs = [(i, j) for i in range(blocks) for j in range(i, blocks)]
    Z = F // 2
    slots = F * slot
    c = lax.axis_index("coarse")
    f = lax.axis_index("fine")
    core = lax.rem(f, 2)
    z = lax.div(f, 2)
    sibling = (c, f + 1 - 2 * core)

    def fine_peer(k):
        return lax.rem(f + k, F)

    def coarse_peer(k):
        return lax.rem(c + k, C)

    def z_peer(k):
        return lax.rem(z + k, Z)

    def z_other(k, flip):
        return 2 * z_peer(k) + (1 - core if flip else core)

    steps = sorted(range(1, Z), key=lambda k: -min(k, Z - k))
    far = [z_other(steps[0], False)]
    far += [z_other(k, flip) for k in steps[1:] for flip in (False, True)]
    far += [z_other(steps[0], True)]
    cuts = [0, len(far) // 6, len(far) // 3, 2 * len(far) // 3, len(far)]
    lots = [far[cuts[n]:cuts[n + 1]] for n in range(4)]
    lots[0].append(z_other(0, True))
    peers = sum(lots, [])

    barrier = pltpu.get_barrier_semaphore()
    for k in range(1, F):
        pl.semaphore_signal(barrier, inc=1, device_id=(c, fine_peer(k)), device_id_type=MESH)
    for k in range(1, C):
        pl.semaphore_signal(barrier, inc=1, device_id=(coarse_peer(k), f), device_id_type=MESH)

    emb_copy.wait()
    used = len(pairs) * LANES
    if stack_rows > used:
        acc[used:, :] = jnp.zeros((stack_rows - used, LANES), jnp.float32)
    place = 0
    for i in range(blocks):
        strip = lax.dot_general(
            emb[:, i * LANES:(i + 1) * LANES], emb[:, i * LANES:],
            (((0,), (0,)), ((), ())), preferred_element_type=jnp.float32,
        )
        for j in range(blocks - i):
            acc[place * LANES:(place + 1) * LANES, :] = strip[:, j * LANES:(j + 1) * LANES]
            place += 1
    pl.semaphore_wait(barrier, F + C - 2)

    half_rows = stack_rows // 2
    part_rows = half_rows // C
    piece_rows = part_rows // Z

    core_copy = remote(
        rows_at(acc, (1 - core) * half_rows, half_rows), half_in, core_s, core_r, sibling
    )
    core_copy.start()

    labels_copy.wait()
    label_row = labels[...]
    onehot = lax.broadcasted_iota(jnp.int32, (F, rows), 0) == label_row
    before = (
        lax.broadcasted_iota(jnp.int32, (rows, rows), 0)
        < lax.broadcasted_iota(jnp.int32, (rows, rows), 1)
    )
    flags = jnp.where(onehot, 1.0, 0.0)
    rank_all = dot(flags.astype(jnp.bfloat16), jnp.where(before, 1.0, 0.0).astype(jnp.bfloat16))
    rank = jnp.sum(jnp.where(onehot, rank_all, 0.0), axis=0, keepdims=True).astype(jnp.int32)
    amounts = jnp.sum(flags, axis=1, keepdims=True)
    for label in range(F):
        counts_out[label] = jnp.broadcast_to(amounts[label:label + 1, :], (8, LANES))
    slot_of = label_row * slot + rank
    def slot_rows(ref, which):
        return ref.at[pl.ds(pl.multiple_of(which * slot, 16), slot)]

    def row_copy(to, source):
        return remote(
            slot_rows(outgoing, to), slot_rows(received, source), a_s.at[to], a_r.at[source], (c, to)
        )

    def count_copy(to, source):
        return remote(counts_out.at[to], counts_in.at[source], n_s.at[to], n_r.at[source], (c, to))

    def compact(devices):
        places = lax.broadcasted_iota(jnp.int32, (slot, rows), 0)
        picks = [
            jnp.where(places + to * slot == slot_of, 1.0, 0.0).astype(jnp.bfloat16) for to in devices
        ]
        picked = dot(jnp.concatenate(picks, axis=0), emb[...]).astype(jnp.bfloat16)
        for n, to in enumerate(devices):
            slot_rows(outgoing, to)[...] = picked[n * slot:(n + 1) * slot, :]

    compact(lots[0])

    core_copy.wait_recv()
    half[...] = rows_at(acc, core * half_rows, half_rows)[...] + half_in[...]

    def coarse_copy(to, source):
        return remote(
            rows_at(half, to * part_rows, part_rows), coarse_in.at[source],
            coarse_s.at[to], coarse_r.at[source], (to, f),
        )

    for k in range(1, C):
        coarse_copy(coarse_peer(k), c).start()
    for peer in lots[0]:
        row_copy(peer, f).start()
    for peer in peers:
        count_copy(peer, f).start()
    compact(lots[1] + lots[2] + lots[3] + [f])
    slot_rows(received, f)[...] = slot_rows(outgoing, f)[...]
    counts_in[f] = counts_out[f]
    value = rows_at(half, c * part_rows, part_rows)[...]
    for k in range(1, C):
        coarse_copy(coarse_peer(k), coarse_peer(k)).wait_recv()
        value = value + coarse_in[coarse_peer(k)]
    part[...] = value

    def z_copy(to, source):
        return remote(
            rows_at(part, to * piece_rows, piece_rows), z_in.at[source],
            z_s.at[to], z_r.at[source], (c, 2 * to + core),
        )

    for k in range(1, Z):
        z_copy(z_peer(k), z).start()
    for peer in lots[1]:
        row_copy(peer, f).start()
    value = rows_at(part, z * piece_rows, piece_rows)[...]
    for k in range(1, Z):
        z_copy(z_peer(k), z_peer(k)).wait_recv()
        value = value + z_in[z_peer(k)]

    def piece_start(coarse_id, z_id):
        return core * half_rows + coarse_id * part_rows + z_id * piece_rows

    rows_at(total, piece_start(c, z), piece_rows)[...] = value

    def z_gather(to, source):
        piece = rows_at(total, piece_start(c, source), piece_rows)
        return remote(piece, piece, gz_s.at[to], gz_r.at[source], (c, 2 * to + core))

    def coarse_gather(to, source):
        piece = rows_at(total, piece_start(source, 0), part_rows)
        return remote(piece, piece, gc_s.at[to], gc_r.at[source], (to, f))

    def core_gather(source):
        piece = rows_at(total, source * half_rows, half_rows)
        return remote(piece, piece, gk_s, gk_r, sibling)

    for k in range(1, Z):
        z_gather(z_peer(k), z).start()
    for k in range(1, Z):
        z_gather(z_peer(k), z_peer(k)).wait_recv()
    for k in range(1, C):
        coarse_gather(coarse_peer(k), c).start()
    for peer in lots[2]:
        row_copy(peer, f).start()
    for k in range(1, C):
        coarse_gather(coarse_peer(k), coarse_peer(k)).wait_recv()
    core_gather(core).start()
    for peer in lots[3]:
        row_copy(peer, f).start()

    for k in range(1, F):
        count_copy(fine_peer(k), fine_peer(k)).wait_recv()

    core_gather(1 - core).wait_recv()
    for place, (i, j) in enumerate(pairs):
        block = total[place * LANES:(place + 1) * LANES, :] * (1.0 / row_total)
        if i == j:
            diagonal = (
                lax.broadcasted_iota(jnp.int32, (LANES, LANES), 0)
                == lax.broadcasted_iota(jnp.int32, (LANES, LANES), 1)
            )
            block = block + jnp.where(diagonal, RIDGE, 0.0)
        else:
            full[j * LANES:(j + 1) * LANES, i * LANES:(i + 1) * LANES] = block.T
        full[i * LANES:(i + 1) * LANES, j * LANES:(j + 1) * LANES] = block
    second = full[...]
    norm_scale = jnp.max(jnp.sum(jnp.abs(second), axis=0, keepdims=True), axis=1, keepdims=True)
    root = second * (1.0 / norm_scale)
    identity = jnp.where(
        lax.broadcasted_iota(jnp.int32, (width, width), 0)
        == lax.broadcasted_iota(jnp.int32, (width, width), 1),
        2.25, 0.0,
    )
    root_b = root.astype(jnp.bfloat16)
    square = dot(root_b, root_b)
    outer = (0.0625 * square - 0.5625 * root).astype(jnp.bfloat16)
    inverse = identity - 2.4375 * root + 1.6875 * square + dot(square.astype(jnp.bfloat16), outer)
    whiten[...] = (inverse * (1.0 / jnp.sqrt(norm_scale))).astype(jnp.bfloat16)

    group = LANES // slot
    if group == 1:
        batches = [[f] + lots[0] + lots[1] + lots[2], lots[3]]
    else:
        batches = [[lax.rem(lax.div(f, group) + n, F // group) for n in range(F // group)]]
        for peer in peers:
            row_copy(peer, peer).wait_recv()
    order = sum(batches, [])
    rank_here = lax.broadcasted_iota(jnp.int32, (slot, LANES), 0).astype(jnp.float32)
    diagonal = (
        lax.broadcasted_iota(jnp.int32, (LANES, LANES), 0)
        == lax.broadcasted_iota(jnp.int32, (LANES, LANES), 1)
    )

    def highest(tile):
        return jnp.max(tile.reshape(LANES // 8, 8, LANES), axis=0)

    tops, biases, done = [], [], 0
    for batch in batches:
        if group == 1:
            for block in batch:
                if block is not f:
                    row_copy(block, block).wait_recv()
        arrived = [rows_at(received, block * LANES, LANES)[...] for block in batch]
        white = dot(jnp.concatenate(arrived, axis=0), whiten[...])
        meansq = jnp.mean(white * white, axis=-1, keepdims=True)
        here = (white * lax.rsqrt(width * (meansq + EPS))).astype(jnp.bfloat16)
        end = done + len(batch)
        unit[done * LANES:end * LANES, :] = here
        for block in batch:
            bias = [
                jnp.where(rank_here < counts_in[block * group + m][0:1, :], 0.0, LOW) for m in range(group)
            ]
            biases.append(bias[0] if group == 1 else jnp.concatenate(bias, axis=0))
            tops.append(jnp.full((8, LANES), -1.0, jnp.float32))
        down = lax.dot_general(
            here, unit[0:end * LANES, :], (((1,), (1,)), ((), ())), preferred_element_type=jnp.float32
        )
        for q in range(done, end):
            for t in range(end):
                tile = down[(q - done) * LANES:(q - done + 1) * LANES, t * LANES:(t + 1) * LANES] + biases[q]
                if t == q:
                    tile = jnp.where(diagonal, LOW, tile)
                tops[t] = jnp.maximum(tops[t], highest(tile))
        if done > 0:
            across = lax.dot_general(
                unit[0:done * LANES, :], here, (((1,), (1,)), ((), ())), preferred_element_type=jnp.float32
            )
            for q in range(done):
                for t in range(done, end):
                    tile = across[q * LANES:(q + 1) * LANES, (t - done) * LANES:(t - done + 1) * LANES]
                    tops[t] = jnp.maximum(tops[t], highest(tile + biases[q]))
        done = end
    for n, block in enumerate(order):
        best[block] = jnp.broadcast_to(jnp.max(tops[n], axis=0, keepdims=True), (8, LANES))

    def best_copy(to, source):
        return remote(
            best.at[lax.div(to, group)], returned.at[source], b_s.at[to], b_r.at[source], (c, to)
        )

    for peer in peers:
        best_copy(peer, f).start()
    returned[f] = best[lax.div(f, group)]
    pick = lax.broadcasted_iota(jnp.int32, (LANES, rows), 0) == rank + lax.rem(f * slot, LANES)
    pick = jnp.where(pick, 1.0, 0.0).astype(jnp.bfloat16)
    mine = lax.broadcasted_iota(jnp.int32, (F * 8, rows), 0) == label_row * 8
    for k in range(1, F):
        best_copy(fine_peer(k), fine_peer(k)).wait_recv()
    values = returned[...].reshape(F * 8, LANES)
    high, rest = values.astype(jnp.bfloat16), None
    rest = values - high.astype(jnp.float32)
    middle, low = split_two(rest)
    found = dot(high, pick) + (dot(middle, pick) + dot(low, pick))
    out[...] = jnp.sum(jnp.where(mine, found, 0.0), axis=0, keepdims=True)

    core_copy.wait_send()
    core_gather(core).wait_send()
    for k in range(1, C):
        coarse_copy(coarse_peer(k), c).wait_send()
        coarse_gather(coarse_peer(k), c).wait_send()
    for k in range(1, Z):
        z_copy(z_peer(k), z).wait_send()
        z_gather(z_peer(k), z).wait_send()
    for k in range(1, F):
        row_copy(fine_peer(k), f).wait_send()
        count_copy(fine_peer(k), f).wait_send()
        best_copy(fine_peer(k), f).wait_send()


def per_device(embeddings, labels):
    rows, width = embeddings.shape
    F = lax.axis_size("fine")
    C = lax.axis_size("coarse")
    Z = F // 2
    slot = 2 * rows // F
    slots = F * slot
    blocks = width // LANES
    unit_rows = 8 * C * F
    stack_rows = -(-(blocks * (blocks + 1) // 2 * LANES) // unit_rows) * unit_rows
    half_rows = stack_rows // 2
    part_rows = half_rows // C
    piece_rows = part_rows // Z
    f32, bf16 = jnp.float32, jnp.bfloat16
    dma = pltpu.SemaphoreType.DMA
    best = pl.pallas_call(
        functools.partial(kernel, C, F, slot, stack_rows, rows * F * C),
        out_shape=jax.ShapeDtypeStruct((1, rows), f32),
        in_specs=[pl.BlockSpec(memory_space=pl.ANY)] * 2,
        out_specs=pl.BlockSpec(memory_space=pltpu.VMEM),
        scratch_shapes=[
            pltpu.VMEM((rows, width), bf16),
            pltpu.VMEM((1, rows), jnp.int32),
            pltpu.VMEM((stack_rows, LANES), f32),
            pltpu.VMEM((half_rows, LANES), f32),
            pltpu.VMEM((half_rows, LANES), f32),
            pltpu.VMEM((C, part_rows, LANES), f32),
            pltpu.VMEM((part_rows, LANES), f32),
            pltpu.VMEM((Z, piece_rows, LANES), f32),
            pltpu.VMEM((stack_rows, LANES), f32),
            pltpu.VMEM((slots, width), bf16),
            pltpu.VMEM((slots, width), bf16),
            pltpu.VMEM((F, 8, LANES), f32),
            pltpu.VMEM((F, 8, LANES), f32),
            pltpu.VMEM((width, width), f32),
            pltpu.VMEM((width, width), bf16),
            pltpu.VMEM((slots, width), bf16),
            pltpu.VMEM((slots // LANES, 8, LANES), f32),
            pltpu.VMEM((F, 8, LANES), f32),
            dma, dma,
            dma, dma, dma((C,)), dma((C,)), dma((Z,)), dma((Z,)),
            dma((Z,)), dma((Z,)), dma((C,)), dma((C,)), dma, dma,
            dma((F,)), dma((F,)), dma((F,)), dma((F,)), dma((F,)), dma((F,)),
        ],
        compiler_params=pltpu.CompilerParams(
            collective_id=0, has_side_effects=True, vmem_limit_bytes=(64 * 1024 - 256) * 1024
        ),
    )(embeddings, labels.reshape(1, rows))
    return best.reshape(rows)


def solution(mesh):
    in_specs = (P(("coarse", "fine"), None), P(("coarse", "fine"), None))
    out_specs = P(("coarse", "fine"))
    return jax.shard_map(
        per_device, mesh=mesh, in_specs=in_specs, out_specs=out_specs, check_vma=False
    )
```

```python
import functools

import jax
import jax.numpy as jnp
from jax import lax
from jax.experimental import pallas as pl
from jax.experimental.pallas import tpu as pltpu
from jax.sharding import PartitionSpec as P

EPS = 1e-06
RIDGE = 0.001
LANES = 128
LOW = -3.0e38
MESH = pl.DeviceIdType.MESH


def dot(left, right):
    return jnp.dot(left, right, preferred_element_type=jnp.float32)


def split_two(value):
    high = value.astype(jnp.bfloat16)
    return high, (value - high.astype(jnp.float32)).astype(jnp.bfloat16)


def remote(src, dst, send_sem, recv_sem, device):
    return pltpu.make_async_remote_copy(
        src_ref=src, dst_ref=dst, send_sem=send_sem, recv_sem=recv_sem,
        device_id=device, device_id_type=MESH,
    )


def rows_at(ref, start, size):
    return ref.at[pl.ds(pl.multiple_of(start, 8), size)]


def kernel(
    C, F, slot, stack_rows, row_total,
    emb_hbm, labels_hbm, out,
    emb, labels, acc, half_in, half, coarse_in, part, z_in, total,
    outgoing, received, counts_out, counts_in, full, whiten, unit, best, returned,
    emb_sem, labels_sem,    core_s, core_r, coarse_s, coarse_r, z_s, z_r, gz_s, gz_r, gc_s, gc_r, gk_s, gk_r,
    a_s, a_r, n_s, n_r, b_s, b_r,
):
    emb_copy = pltpu.make_async_copy(emb_hbm, emb, emb_sem)
    labels_copy = pltpu.make_async_copy(labels_hbm, labels, labels_sem)
    emb_copy.start()
    labels_copy.start()
    rows, width = emb.shape
    blocks = width // LANES
    pairs = [(i, j) for i in range(blocks) for j in range(i, blocks)]
    Z = F // 2
    slots = F * slot
    c = lax.axis_index("coarse")
    f = lax.axis_index("fine")
    core = lax.rem(f, 2)
    z = lax.div(f, 2)
    sibling = (c, f + 1 - 2 * core)

    def fine_peer(k):
        return lax.rem(f + k, F)

    def coarse_peer(k):
        return lax.rem(c + k, C)

    def z_peer(k):
        return lax.rem(z + k, Z)

    def z_other(k, flip):
        return 2 * z_peer(k) + (1 - core if flip else core)

    steps = sorted(range(1, Z), key=lambda k: -min(k, Z - k))
    far = [z_other(steps[0], False)]
    far += [z_other(k, flip) for k in steps[1:] for flip in (False, True)]
    far += [z_other(steps[0], True)]
    cuts = [0, len(far) // 6, len(far) // 2, 5 * len(far) // 6, len(far)]
    lots = [far[cuts[n]:cuts[n + 1]] for n in range(4)]
    lots[0].append(z_other(0, True))
    peers = sum(lots, [])

    barrier = pltpu.get_barrier_semaphore()
    for k in range(1, F):
        pl.semaphore_signal(barrier, inc=1, device_id=(c, fine_peer(k)), device_id_type=MESH)
    for k in range(1, C):
        pl.semaphore_signal(barrier, inc=1, device_id=(coarse_peer(k), f), device_id_type=MESH)

    emb_copy.wait()
    used = len(pairs) * LANES
    if stack_rows > used:
        acc[used:, :] = jnp.zeros((stack_rows - used, LANES), jnp.float32)
    place = 0
    for i in range(blocks):
        strip = lax.dot_general(
            emb[:, i * LANES:(i + 1) * LANES], emb[:, i * LANES:],
            (((0,), (0,)), ((), ())), preferred_element_type=jnp.float32,
        )
        for j in range(blocks - i):
            acc[place * LANES:(place + 1) * LANES, :] = strip[:, j * LANES:(j + 1) * LANES]
            place += 1
    pl.semaphore_wait(barrier, F + C - 2)

    half_rows = stack_rows // 2
    part_rows = half_rows // C
    piece_rows = part_rows // Z

    core_copy = remote(
        rows_at(acc, (1 - core) * half_rows, half_rows), half_in, core_s, core_r, sibling
    )
    core_copy.start()

    labels_copy.wait()
    label_row = labels[...]
    onehot = lax.broadcasted_iota(jnp.int32, (F, rows), 0) == label_row
    before = (
        lax.broadcasted_iota(jnp.int32, (rows, rows), 0)
        < lax.broadcasted_iota(jnp.int32, (rows, rows), 1)
    )
    flags = jnp.where(onehot, 1.0, 0.0)
    rank_all = dot(flags.astype(jnp.bfloat16), jnp.where(before, 1.0, 0.0).astype(jnp.bfloat16))
    rank = jnp.sum(jnp.where(onehot, rank_all, 0.0), axis=0, keepdims=True).astype(jnp.int32)
    amounts = jnp.sum(flags, axis=1, keepdims=True)
    for label in range(F):
        counts_out[label] = jnp.broadcast_to(amounts[label:label + 1, :], (8, LANES))
    slot_of = label_row * slot + rank
    def slot_rows(ref, which):
        return ref.at[pl.ds(pl.multiple_of(which * slot, 16), slot)]

    def row_copy(to, source):
        return remote(
            slot_rows(outgoing, to), slot_rows(received, source), a_s.at[to], a_r.at[source], (c, to)
        )

    def count_copy(to, source):
        return remote(counts_out.at[to], counts_in.at[source], n_s.at[to], n_r.at[source], (c, to))

    def compact(devices):
        places = lax.broadcasted_iota(jnp.int32, (slot, rows), 0)
        picks = [
            jnp.where(places + to * slot == slot_of, 1.0, 0.0).astype(jnp.bfloat16) for to in devices
        ]
        picked = dot(jnp.concatenate(picks, axis=0), emb[...]).astype(jnp.bfloat16)
        for n, to in enumerate(devices):
            slot_rows(outgoing, to)[...] = picked[n * slot:(n + 1) * slot, :]

    core_copy.wait_recv()
    half[...] = rows_at(acc, core * half_rows, half_rows)[...] + half_in[...]

    def coarse_copy(to, source):
        return remote(
            rows_at(half, to * part_rows, part_rows), coarse_in.at[source],
            coarse_s.at[to], coarse_r.at[source], (to, f),
        )

    for k in range(1, C):
        coarse_copy(coarse_peer(k), c).start()
    compact(lots[0])
    for peer in lots[0]:
        row_copy(peer, f).start()
    for peer in peers:
        count_copy(peer, f).start()
    compact(lots[1] + lots[2] + lots[3] + [f])
    slot_rows(received, f)[...] = slot_rows(outgoing, f)[...]
    counts_in[f] = counts_out[f]
    value = rows_at(half, c * part_rows, part_rows)[...]
    for k in range(1, C):
        coarse_copy(coarse_peer(k), coarse_peer(k)).wait_recv()
        value = value + coarse_in[coarse_peer(k)]
    part[...] = value

    def z_copy(to, source):
        return remote(
            rows_at(part, to * piece_rows, piece_rows), z_in.at[source],
            z_s.at[to], z_r.at[source], (c, 2 * to + core),
        )

    for k in range(1, Z):
        z_copy(z_peer(k), z).start()
    for peer in lots[1]:
        row_copy(peer, f).start()
    value = rows_at(part, z * piece_rows, piece_rows)[...]
    for k in range(1, Z):
        z_copy(z_peer(k), z_peer(k)).wait_recv()
        value = value + z_in[z_peer(k)]

    def piece_start(coarse_id, z_id):
        return core * half_rows + coarse_id * part_rows + z_id * piece_rows

    rows_at(total, piece_start(c, z), piece_rows)[...] = value

    def z_gather(to, source):
        piece = rows_at(total, piece_start(c, source), piece_rows)
        return remote(piece, piece, gz_s.at[to], gz_r.at[source], (c, 2 * to + core))

    def coarse_gather(to, source):
        piece = rows_at(total, piece_start(source, 0), part_rows)
        return remote(piece, piece, gc_s.at[to], gc_r.at[source], (to, f))

    def core_gather(source):
        piece = rows_at(total, source * half_rows, half_rows)
        return remote(piece, piece, gk_s, gk_r, sibling)

    for k in range(1, Z):
        z_gather(z_peer(k), z).start()
    for k in range(1, Z):
        z_gather(z_peer(k), z_peer(k)).wait_recv()
    for k in range(1, C):
        coarse_gather(coarse_peer(k), c).start()
    for peer in lots[2]:
        row_copy(peer, f).start()
    for k in range(1, C):
        coarse_gather(coarse_peer(k), coarse_peer(k)).wait_recv()
    core_gather(core).start()
    for peer in lots[3]:
        row_copy(peer, f).start()

    for k in range(1, F):
        count_copy(fine_peer(k), fine_peer(k)).wait_recv()

    core_gather(1 - core).wait_recv()
    for place, (i, j) in enumerate(pairs):
        block = total[place * LANES:(place + 1) * LANES, :] * (1.0 / row_total)
        if i == j:
            diagonal = (
                lax.broadcasted_iota(jnp.int32, (LANES, LANES), 0)
                == lax.broadcasted_iota(jnp.int32, (LANES, LANES), 1)
            )
            block = block + jnp.where(diagonal, RIDGE, 0.0)
        else:
            full[j * LANES:(j + 1) * LANES, i * LANES:(i + 1) * LANES] = block.T
        full[i * LANES:(i + 1) * LANES, j * LANES:(j + 1) * LANES] = block
    second = full[...]
    norm_scale = jnp.max(jnp.sum(jnp.abs(second), axis=0, keepdims=True), axis=1, keepdims=True)
    root = second * (1.0 / norm_scale)
    identity = jnp.where(
        lax.broadcasted_iota(jnp.int32, (width, width), 0)
        == lax.broadcasted_iota(jnp.int32, (width, width), 1),
        2.25, 0.0,
    )
    root_b = root.astype(jnp.bfloat16)
    square = dot(root_b, root_b)
    outer = (0.0625 * square - 0.5625 * root).astype(jnp.bfloat16)
    inverse = identity - 2.4375 * root + 1.6875 * square + dot(square.astype(jnp.bfloat16), outer)
    whiten[...] = (inverse * (1.0 / jnp.sqrt(norm_scale))).astype(jnp.bfloat16)

    group = LANES // slot
    if group == 1:
        batches = [[f] + lots[0] + lots[1] + lots[2], lots[3]]
    else:
        batches = [[lax.rem(lax.div(f, group) + n, F // group) for n in range(F // group)]]
        for peer in peers:
            row_copy(peer, peer).wait_recv()
    order = sum(batches, [])
    rank_here = lax.broadcasted_iota(jnp.int32, (slot, LANES), 0).astype(jnp.float32)
    diagonal = (
        lax.broadcasted_iota(jnp.int32, (LANES, LANES), 0)
        == lax.broadcasted_iota(jnp.int32, (LANES, LANES), 1)
    )

    def highest(tile):
        return jnp.max(tile.reshape(LANES // 8, 8, LANES), axis=0)

    tops, biases, done = [], [], 0
    for batch in batches:
        if group == 1:
            for block in batch:
                if block is not f:
                    row_copy(block, block).wait_recv()
        arrived = [rows_at(received, block * LANES, LANES)[...] for block in batch]
        white = dot(jnp.concatenate(arrived, axis=0), whiten[...])
        meansq = jnp.mean(white * white, axis=-1, keepdims=True)
        here = (white * lax.rsqrt(width * (meansq + EPS))).astype(jnp.bfloat16)
        end = done + len(batch)
        unit[done * LANES:end * LANES, :] = here
        for block in batch:
            bias = [
                jnp.where(rank_here < counts_in[block * group + m][0:1, :], 0.0, LOW) for m in range(group)
            ]
            biases.append(bias[0] if group == 1 else jnp.concatenate(bias, axis=0))
            tops.append(jnp.full((8, LANES), -1.0, jnp.float32))
        down = lax.dot_general(
            here, unit[0:end * LANES, :], (((1,), (1,)), ((), ())), preferred_element_type=jnp.float32
        )
        for q in range(done, end):
            for t in range(end):
                tile = down[(q - done) * LANES:(q - done + 1) * LANES, t * LANES:(t + 1) * LANES] + biases[q]
                if t == q:
                    tile = jnp.where(diagonal, LOW, tile)
                tops[t] = jnp.maximum(tops[t], highest(tile))
        if done > 0:
            across = lax.dot_general(
                unit[0:done * LANES, :], here, (((1,), (1,)), ((), ())), preferred_element_type=jnp.float32
            )
            for q in range(done):
                for t in range(done, end):
                    tile = across[q * LANES:(q + 1) * LANES, (t - done) * LANES:(t - done + 1) * LANES]
                    tops[t] = jnp.maximum(tops[t], highest(tile + biases[q]))
        done = end
    for n, block in enumerate(order):
        best[block] = jnp.broadcast_to(jnp.max(tops[n], axis=0, keepdims=True), (8, LANES))

    def best_copy(to, source):
        return remote(
            best.at[lax.div(to, group)], returned.at[source], b_s.at[to], b_r.at[source], (c, to)
        )

    for peer in peers:
        best_copy(peer, f).start()
    returned[f] = best[lax.div(f, group)]
    pick = lax.broadcasted_iota(jnp.int32, (LANES, rows), 0) == rank + lax.rem(f * slot, LANES)
    pick = jnp.where(pick, 1.0, 0.0).astype(jnp.bfloat16)
    mine = lax.broadcasted_iota(jnp.int32, (F * 8, rows), 0) == label_row * 8
    for k in range(1, F):
        best_copy(fine_peer(k), fine_peer(k)).wait_recv()
    values = returned[...].reshape(F * 8, LANES)
    high, rest = values.astype(jnp.bfloat16), None
    rest = values - high.astype(jnp.float32)
    middle, low = split_two(rest)
    found = dot(high, pick) + (dot(middle, pick) + dot(low, pick))
    out[...] = jnp.sum(jnp.where(mine, found, 0.0), axis=0, keepdims=True)

    core_copy.wait_send()
    core_gather(core).wait_send()
    for k in range(1, C):
        coarse_copy(coarse_peer(k), c).wait_send()
        coarse_gather(coarse_peer(k), c).wait_send()
    for k in range(1, Z):
        z_copy(z_peer(k), z).wait_send()
        z_gather(z_peer(k), z).wait_send()
    for k in range(1, F):
        row_copy(fine_peer(k), f).wait_send()
        count_copy(fine_peer(k), f).wait_send()
        best_copy(fine_peer(k), f).wait_send()


def per_device(embeddings, labels):
    rows, width = embeddings.shape
    F = lax.axis_size("fine")
    C = lax.axis_size("coarse")
    Z = F // 2
    slot = 2 * rows // F
    slots = F * slot
    blocks = width // LANES
    unit_rows = 8 * C * F
    stack_rows = -(-(blocks * (blocks + 1) // 2 * LANES) // unit_rows) * unit_rows
    half_rows = stack_rows // 2
    part_rows = half_rows // C
    piece_rows = part_rows // Z
    f32, bf16 = jnp.float32, jnp.bfloat16
    dma = pltpu.SemaphoreType.DMA
    best = pl.pallas_call(
        functools.partial(kernel, C, F, slot, stack_rows, rows * F * C),
        out_shape=jax.ShapeDtypeStruct((1, rows), f32),
        in_specs=[pl.BlockSpec(memory_space=pl.ANY)] * 2,
        out_specs=pl.BlockSpec(memory_space=pltpu.VMEM),
        scratch_shapes=[
            pltpu.VMEM((rows, width), bf16),
            pltpu.VMEM((1, rows), jnp.int32),
            pltpu.VMEM((stack_rows, LANES), f32),
            pltpu.VMEM((half_rows, LANES), f32),
            pltpu.VMEM((half_rows, LANES), f32),
            pltpu.VMEM((C, part_rows, LANES), f32),
            pltpu.VMEM((part_rows, LANES), f32),
            pltpu.VMEM((Z, piece_rows, LANES), f32),
            pltpu.VMEM((stack_rows, LANES), f32),
            pltpu.VMEM((slots, width), bf16),
            pltpu.VMEM((slots, width), bf16),
            pltpu.VMEM((F, 8, LANES), f32),
            pltpu.VMEM((F, 8, LANES), f32),
            pltpu.VMEM((width, width), f32),
            pltpu.VMEM((width, width), bf16),
            pltpu.VMEM((slots, width), bf16),
            pltpu.VMEM((slots // LANES, 8, LANES), f32),
            pltpu.VMEM((F, 8, LANES), f32),
            dma, dma,
            dma, dma, dma((C,)), dma((C,)), dma((Z,)), dma((Z,)),
            dma((Z,)), dma((Z,)), dma((C,)), dma((C,)), dma, dma,
            dma((F,)), dma((F,)), dma((F,)), dma((F,)), dma((F,)), dma((F,)),
        ],
        compiler_params=pltpu.CompilerParams(
            collective_id=0, has_side_effects=True, vmem_limit_bytes=(64 * 1024 - 256) * 1024
        ),
    )(embeddings, labels.reshape(1, rows))
    return best.reshape(rows)


def solution(mesh):
    in_specs = (P(("coarse", "fine"), None), P(("coarse", "fine"), None))
    out_specs = P(("coarse", "fine"))
    return jax.shard_map(
        per_device, mesh=mesh, in_specs=in_specs, out_specs=out_specs, check_vma=False
    )
```

```python
import functools

import jax
import jax.numpy as jnp
from jax import lax
from jax.experimental import pallas as pl
from jax.experimental.pallas import tpu as pltpu
from jax.sharding import PartitionSpec as P

EPS = 1e-06
RIDGE = 0.001
LANES = 128
LOW = -3.0e38
MESH = pl.DeviceIdType.MESH


def dot(left, right):
    return jnp.dot(left, right, preferred_element_type=jnp.float32)


def split_two(value):
    high = value.astype(jnp.bfloat16)
    return high, (value - high.astype(jnp.float32)).astype(jnp.bfloat16)


def remote(src, dst, send_sem, recv_sem, device):
    return pltpu.make_async_remote_copy(
        src_ref=src, dst_ref=dst, send_sem=send_sem, recv_sem=recv_sem,
        device_id=device, device_id_type=MESH,
    )


def rows_at(ref, start, size):
    return ref.at[pl.ds(pl.multiple_of(start, 8), size)]


def kernel(
    C, F, slot, stack_rows, row_total,
    emb_hbm, labels_hbm, out,
    emb, labels, acc, half_in, half, coarse_in, part, z_in, total,
    outgoing, received, counts_out, counts_in, full, whiten, unit, best, returned,
    emb_sem, labels_sem,    core_s, core_r, coarse_s, coarse_r, z_s, z_r, gz_s, gz_r, gc_s, gc_r, gk_s, gk_r,
    a_s, a_r, n_s, n_r, b_s, b_r,
):
    emb_copy = pltpu.make_async_copy(emb_hbm, emb, emb_sem)
    labels_copy = pltpu.make_async_copy(labels_hbm, labels, labels_sem)
    emb_copy.start()
    labels_copy.start()
    rows, width = emb.shape
    blocks = width // LANES
    pairs = [(i, j) for i in range(blocks) for j in range(i, blocks)]
    Z = F // 2
    slots = F * slot
    c = lax.axis_index("coarse")
    f = lax.axis_index("fine")
    core = lax.rem(f, 2)
    z = lax.div(f, 2)
    sibling = (c, f + 1 - 2 * core)

    def fine_peer(k):
        return lax.rem(f + k, F)

    def coarse_peer(k):
        return lax.rem(c + k, C)

    def z_peer(k):
        return lax.rem(z + k, Z)

    def z_other(k, flip):
        return 2 * z_peer(k) + (1 - core if flip else core)

    steps = sorted(range(1, Z), key=lambda k: -min(k, Z - k))
    far = [z_other(steps[0], False)]
    far += [z_other(k, flip) for k in steps[1:] for flip in (False, True)]
    far += [z_other(steps[0], True)]
    cuts = [0, len(far) // 6, 2 * len(far) // 3, len(far)]
    lots = [far[cuts[n]:cuts[n + 1]] for n in range(3)]
    lots[0].append(z_other(0, True))
    peers = sum(lots, [])

    barrier = pltpu.get_barrier_semaphore()
    for k in range(1, F):
        pl.semaphore_signal(barrier, inc=1, device_id=(c, fine_peer(k)), device_id_type=MESH)
    for k in range(1, C):
        pl.semaphore_signal(barrier, inc=1, device_id=(coarse_peer(k), f), device_id_type=MESH)

    emb_copy.wait()
    used = len(pairs) * LANES
    if stack_rows > used:
        acc[used:, :] = jnp.zeros((stack_rows - used, LANES), jnp.float32)
    place = 0
    for i in range(blocks):
        strip = lax.dot_general(
            emb[:, i * LANES:(i + 1) * LANES], emb[:, i * LANES:],
            (((0,), (0,)), ((), ())), preferred_element_type=jnp.float32,
        )
        for j in range(blocks - i):
            acc[place * LANES:(place + 1) * LANES, :] = strip[:, j * LANES:(j + 1) * LANES]
            place += 1
    pl.semaphore_wait(barrier, F + C - 2)

    half_rows = stack_rows // 2
    part_rows = half_rows // C
    piece_rows = part_rows // Z

    core_copy = remote(
        rows_at(acc, (1 - core) * half_rows, half_rows), half_in, core_s, core_r, sibling
    )
    core_copy.start()

    labels_copy.wait()
    label_row = labels[...]
    onehot = lax.broadcasted_iota(jnp.int32, (F, rows), 0) == label_row
    before = (
        lax.broadcasted_iota(jnp.int32, (rows, rows), 0)
        < lax.broadcasted_iota(jnp.int32, (rows, rows), 1)
    )
    flags = jnp.where(onehot, 1.0, 0.0)
    rank_all = dot(flags.astype(jnp.bfloat16), jnp.where(before, 1.0, 0.0).astype(jnp.bfloat16))
    rank = jnp.sum(jnp.where(onehot, rank_all, 0.0), axis=0, keepdims=True).astype(jnp.int32)
    amounts = jnp.sum(flags, axis=1, keepdims=True)
    for label in range(F):
        counts_out[label] = jnp.broadcast_to(amounts[label:label + 1, :], (8, LANES))
    slot_of = label_row * slot + rank
    def slot_rows(ref, which):
        return ref.at[pl.ds(pl.multiple_of(which * slot, 16), slot)]

    def row_copy(to, source):
        return remote(
            slot_rows(outgoing, to), slot_rows(received, source), a_s.at[to], a_r.at[source], (c, to)
        )

    def count_copy(to, source):
        return remote(counts_out.at[to], counts_in.at[source], n_s.at[to], n_r.at[source], (c, to))

    def compact(devices):
        places = lax.broadcasted_iota(jnp.int32, (slot, rows), 0)
        picks = [
            jnp.where(places + to * slot == slot_of, 1.0, 0.0).astype(jnp.bfloat16) for to in devices
        ]
        picked = dot(jnp.concatenate(picks, axis=0), emb[...]).astype(jnp.bfloat16)
        for n, to in enumerate(devices):
            slot_rows(outgoing, to)[...] = picked[n * slot:(n + 1) * slot, :]

    compact(lots[0])

    core_copy.wait_recv()
    half[...] = rows_at(acc, core * half_rows, half_rows)[...] + half_in[...]

    def coarse_copy(to, source):
        return remote(
            rows_at(half, to * part_rows, part_rows), coarse_in.at[source],
            coarse_s.at[to], coarse_r.at[source], (to, f),
        )

    for k in range(1, C):
        coarse_copy(coarse_peer(k), c).start()
    for peer in lots[0]:
        row_copy(peer, f).start()
    for peer in peers:
        count_copy(peer, f).start()
    compact(lots[1] + lots[2] + [f])
    slot_rows(received, f)[...] = slot_rows(outgoing, f)[...]
    counts_in[f] = counts_out[f]
    value = rows_at(half, c * part_rows, part_rows)[...]
    for k in range(1, C):
        coarse_copy(coarse_peer(k), coarse_peer(k)).wait_recv()
        value = value + coarse_in[coarse_peer(k)]
    part[...] = value

    def z_copy(to, source):
        return remote(
            rows_at(part, to * piece_rows, piece_rows), z_in.at[source],
            z_s.at[to], z_r.at[source], (c, 2 * to + core),
        )

    for k in range(1, Z):
        z_copy(z_peer(k), z).start()
    value = rows_at(part, z * piece_rows, piece_rows)[...]
    for k in range(1, Z):
        z_copy(z_peer(k), z_peer(k)).wait_recv()
        value = value + z_in[z_peer(k)]

    def piece_start(coarse_id, z_id):
        return core * half_rows + coarse_id * part_rows + z_id * piece_rows

    rows_at(total, piece_start(c, z), piece_rows)[...] = value

    def z_gather(to, source):
        piece = rows_at(total, piece_start(c, source), piece_rows)
        return remote(piece, piece, gz_s.at[to], gz_r.at[source], (c, 2 * to + core))

    def coarse_gather(to, source):
        piece = rows_at(total, piece_start(source, 0), part_rows)
        return remote(piece, piece, gc_s.at[to], gc_r.at[source], (to, f))

    def core_gather(source):
        piece = rows_at(total, source * half_rows, half_rows)
        return remote(piece, piece, gk_s, gk_r, sibling)

    for k in range(1, Z):
        z_gather(z_peer(k), z).start()
    for k in range(1, Z):
        z_gather(z_peer(k), z_peer(k)).wait_recv()
    for k in range(1, C):
        coarse_gather(coarse_peer(k), c).start()
    for peer in lots[1]:
        row_copy(peer, f).start()
    for k in range(1, C):
        coarse_gather(coarse_peer(k), coarse_peer(k)).wait_recv()
    core_gather(core).start()
    for peer in lots[2]:
        row_copy(peer, f).start()

    for k in range(1, F):
        count_copy(fine_peer(k), fine_peer(k)).wait_recv()

    core_gather(1 - core).wait_recv()
    for place, (i, j) in enumerate(pairs):
        block = total[place * LANES:(place + 1) * LANES, :] * (1.0 / row_total)
        if i == j:
            diagonal = (
                lax.broadcasted_iota(jnp.int32, (LANES, LANES), 0)
                == lax.broadcasted_iota(jnp.int32, (LANES, LANES), 1)
            )
            block = block + jnp.where(diagonal, RIDGE, 0.0)
        else:
            full[j * LANES:(j + 1) * LANES, i * LANES:(i + 1) * LANES] = block.T
        full[i * LANES:(i + 1) * LANES, j * LANES:(j + 1) * LANES] = block
    second = full[...]
    norm_scale = jnp.max(jnp.sum(jnp.abs(second), axis=0, keepdims=True), axis=1, keepdims=True)
    root = second * (1.0 / norm_scale)
    identity = jnp.where(
        lax.broadcasted_iota(jnp.int32, (width, width), 0)
        == lax.broadcasted_iota(jnp.int32, (width, width), 1),
        2.25, 0.0,
    )
    root_b = root.astype(jnp.bfloat16)
    square = dot(root_b, root_b)
    outer = (0.0625 * square - 0.5625 * root).astype(jnp.bfloat16)
    inverse = identity - 2.4375 * root + 1.6875 * square + dot(square.astype(jnp.bfloat16), outer)
    whiten[...] = (inverse * (1.0 / jnp.sqrt(norm_scale))).astype(jnp.bfloat16)

    group = LANES // slot
    if group == 1:
        batches = [[f] + lots[0] + lots[1], lots[2]]
    else:
        batches = [[lax.rem(lax.div(f, group) + n, F // group) for n in range(F // group)]]
        for peer in peers:
            row_copy(peer, peer).wait_recv()
    order = sum(batches, [])
    rank_here = lax.broadcasted_iota(jnp.int32, (slot, LANES), 0).astype(jnp.float32)
    diagonal = (
        lax.broadcasted_iota(jnp.int32, (LANES, LANES), 0)
        == lax.broadcasted_iota(jnp.int32, (LANES, LANES), 1)
    )

    def highest(tile):
        return jnp.max(tile.reshape(LANES // 8, 8, LANES), axis=0)

    tops, biases, done = [], [], 0
    for batch in batches:
        if group == 1:
            for block in batch:
                if block is not f:
                    row_copy(block, block).wait_recv()
        arrived = [rows_at(received, block * LANES, LANES)[...] for block in batch]
        white = dot(jnp.concatenate(arrived, axis=0), whiten[...])
        meansq = jnp.mean(white * white, axis=-1, keepdims=True)
        here = (white * lax.rsqrt(width * (meansq + EPS))).astype(jnp.bfloat16)
        end = done + len(batch)
        unit[done * LANES:end * LANES, :] = here
        for block in batch:
            bias = [
                jnp.where(rank_here < counts_in[block * group + m][0:1, :], 0.0, LOW) for m in range(group)
            ]
            biases.append(bias[0] if group == 1 else jnp.concatenate(bias, axis=0))
            tops.append(jnp.full((8, LANES), -1.0, jnp.float32))
        down = lax.dot_general(
            here, unit[0:end * LANES, :], (((1,), (1,)), ((), ())), preferred_element_type=jnp.float32
        )
        for q in range(done, end):
            for t in range(end):
                tile = down[(q - done) * LANES:(q - done + 1) * LANES, t * LANES:(t + 1) * LANES] + biases[q]
                if t == q:
                    tile = jnp.where(diagonal, LOW, tile)
                tops[t] = jnp.maximum(tops[t], highest(tile))
        if done > 0:
            across = lax.dot_general(
                unit[0:done * LANES, :], here, (((1,), (1,)), ((), ())), preferred_element_type=jnp.float32
            )
            for q in range(done):
                for t in range(done, end):
                    tile = across[q * LANES:(q + 1) * LANES, (t - done) * LANES:(t - done + 1) * LANES]
                    tops[t] = jnp.maximum(tops[t], highest(tile + biases[q]))
        done = end
    for n, block in enumerate(order):
        best[block] = jnp.broadcast_to(jnp.max(tops[n], axis=0, keepdims=True), (8, LANES))

    def best_copy(to, source):
        return remote(
            best.at[lax.div(to, group)], returned.at[source], b_s.at[to], b_r.at[source], (c, to)
        )

    for peer in peers:
        best_copy(peer, f).start()
    returned[f] = best[lax.div(f, group)]
    pick = lax.broadcasted_iota(jnp.int32, (LANES, rows), 0) == rank + lax.rem(f * slot, LANES)
    pick = jnp.where(pick, 1.0, 0.0).astype(jnp.bfloat16)
    mine = lax.broadcasted_iota(jnp.int32, (F * 8, rows), 0) == label_row * 8
    for k in range(1, F):
        best_copy(fine_peer(k), fine_peer(k)).wait_recv()
    values = returned[...].reshape(F * 8, LANES)
    high, rest = values.astype(jnp.bfloat16), None
    rest = values - high.astype(jnp.float32)
    middle, low = split_two(rest)
    found = dot(high, pick) + (dot(middle, pick) + dot(low, pick))
    out[...] = jnp.sum(jnp.where(mine, found, 0.0), axis=0, keepdims=True)

    core_copy.wait_send()
    core_gather(core).wait_send()
    for k in range(1, C):
        coarse_copy(coarse_peer(k), c).wait_send()
        coarse_gather(coarse_peer(k), c).wait_send()
    for k in range(1, Z):
        z_copy(z_peer(k), z).wait_send()
        z_gather(z_peer(k), z).wait_send()
    for k in range(1, F):
        row_copy(fine_peer(k), f).wait_send()
        count_copy(fine_peer(k), f).wait_send()
        best_copy(fine_peer(k), f).wait_send()


def per_device(embeddings, labels):
    rows, width = embeddings.shape
    F = lax.axis_size("fine")
    C = lax.axis_size("coarse")
    Z = F // 2
    slot = 2 * rows // F
    slots = F * slot
    blocks = width // LANES
    unit_rows = 8 * C * F
    stack_rows = -(-(blocks * (blocks + 1) // 2 * LANES) // unit_rows) * unit_rows
    half_rows = stack_rows // 2
    part_rows = half_rows // C
    piece_rows = part_rows // Z
    f32, bf16 = jnp.float32, jnp.bfloat16
    dma = pltpu.SemaphoreType.DMA
    best = pl.pallas_call(
        functools.partial(kernel, C, F, slot, stack_rows, rows * F * C),
        out_shape=jax.ShapeDtypeStruct((1, rows), f32),
        in_specs=[pl.BlockSpec(memory_space=pl.ANY)] * 2,
        out_specs=pl.BlockSpec(memory_space=pltpu.VMEM),
        scratch_shapes=[
            pltpu.VMEM((rows, width), bf16),
            pltpu.VMEM((1, rows), jnp.int32),
            pltpu.VMEM((stack_rows, LANES), f32),
            pltpu.VMEM((half_rows, LANES), f32),
            pltpu.VMEM((half_rows, LANES), f32),
            pltpu.VMEM((C, part_rows, LANES), f32),
            pltpu.VMEM((part_rows, LANES), f32),
            pltpu.VMEM((Z, piece_rows, LANES), f32),
            pltpu.VMEM((stack_rows, LANES), f32),
            pltpu.VMEM((slots, width), bf16),
            pltpu.VMEM((slots, width), bf16),
            pltpu.VMEM((F, 8, LANES), f32),
            pltpu.VMEM((F, 8, LANES), f32),
            pltpu.VMEM((width, width), f32),
            pltpu.VMEM((width, width), bf16),
            pltpu.VMEM((slots, width), bf16),
            pltpu.VMEM((slots // LANES, 8, LANES), f32),
            pltpu.VMEM((F, 8, LANES), f32),
            dma, dma,
            dma, dma, dma((C,)), dma((C,)), dma((Z,)), dma((Z,)),
            dma((Z,)), dma((Z,)), dma((C,)), dma((C,)), dma, dma,
            dma((F,)), dma((F,)), dma((F,)), dma((F,)), dma((F,)), dma((F,)),
        ],
        compiler_params=pltpu.CompilerParams(
            collective_id=0, has_side_effects=True, vmem_limit_bytes=(64 * 1024 - 256) * 1024
        ),
    )(embeddings, labels.reshape(1, rows))
    return best.reshape(rows)


def solution(mesh):
    in_specs = (P(("coarse", "fine"), None), P(("coarse", "fine"), None))
    out_specs = P(("coarse", "fine"))
    return jax.shard_map(
        per_device, mesh=mesh, in_specs=in_specs, out_specs=out_specs, check_vma=False
    )
```

```python
import functools

import jax
import jax.numpy as jnp
from jax import lax
from jax.experimental import pallas as pl
from jax.experimental.pallas import tpu as pltpu
from jax.sharding import PartitionSpec as P

EPS = 1e-06
RIDGE = 0.001
LANES = 128
LOW = -3.0e38
MESH = pl.DeviceIdType.MESH


def dot(left, right):
    return jnp.dot(left, right, preferred_element_type=jnp.float32)


def split_two(value):
    high = value.astype(jnp.bfloat16)
    return high, (value - high.astype(jnp.float32)).astype(jnp.bfloat16)


def remote(src, dst, send_sem, recv_sem, device):
    return pltpu.make_async_remote_copy(
        src_ref=src, dst_ref=dst, send_sem=send_sem, recv_sem=recv_sem,
        device_id=device, device_id_type=MESH,
    )


def rows_at(ref, start, size):
    return ref.at[pl.ds(pl.multiple_of(start, 8), size)]


def kernel(
    C, F, slot, stack_rows, row_total,
    emb_hbm, labels_hbm, out,
    emb, labels, acc, half_in, half, coarse_in, part, z_in, total,
    outgoing, received, counts_out, counts_in, full, whiten, unit, best, returned,
    emb_sem, labels_sem,    core_s, core_r, coarse_s, coarse_r, z_s, z_r, gz_s, gz_r, gc_s, gc_r, gk_s, gk_r,
    a_s, a_r, n_s, n_r, b_s, b_r,
):
    emb_copy = pltpu.make_async_copy(emb_hbm, emb, emb_sem)
    labels_copy = pltpu.make_async_copy(labels_hbm, labels, labels_sem)
    emb_copy.start()
    labels_copy.start()
    rows, width = emb.shape
    blocks = width // LANES
    pairs = [(i, j) for i in range(blocks) for j in range(i, blocks)]
    Z = F // 2
    slots = F * slot
    c = lax.axis_index("coarse")
    f = lax.axis_index("fine")
    core = lax.rem(f, 2)
    z = lax.div(f, 2)
    sibling = (c, f + 1 - 2 * core)

    def fine_peer(k):
        return lax.rem(f + k, F)

    def coarse_peer(k):
        return lax.rem(c + k, C)

    def z_peer(k):
        return lax.rem(z + k, Z)

    def z_other(k, flip):
        return 2 * z_peer(k) + (1 - core if flip else core)

    steps = sorted(range(1, Z), key=lambda k: -min(k, Z - k))
    far = [z_other(steps[0], False)]
    far += [z_other(k, flip) for k in steps[1:] for flip in (False, True)]
    far += [z_other(steps[0], True)]
    cuts = [0, len(far) // 6, 5 * len(far) // 6, len(far)]
    lots = [far[cuts[n]:cuts[n + 1]] for n in range(3)]
    lots[0].append(z_other(0, True))
    peers = sum(lots, [])

    barrier = pltpu.get_barrier_semaphore()
    for k in range(1, F):
        pl.semaphore_signal(barrier, inc=1, device_id=(c, fine_peer(k)), device_id_type=MESH)
    for k in range(1, C):
        pl.semaphore_signal(barrier, inc=1, device_id=(coarse_peer(k), f), device_id_type=MESH)

    emb_copy.wait()
    used = len(pairs) * LANES
    if stack_rows > used:
        acc[used:, :] = jnp.zeros((stack_rows - used, LANES), jnp.float32)
    place = 0
    for i in range(blocks):
        strip = lax.dot_general(
            emb[:, i * LANES:(i + 1) * LANES], emb[:, i * LANES:],
            (((0,), (0,)), ((), ())), preferred_element_type=jnp.float32,
        )
        for j in range(blocks - i):
            acc[place * LANES:(place + 1) * LANES, :] = strip[:, j * LANES:(j + 1) * LANES]
            place += 1
    pl.semaphore_wait(barrier, F + C - 2)

    half_rows = stack_rows // 2
    part_rows = half_rows // C
    piece_rows = part_rows // Z

    core_copy = remote(
        rows_at(acc, (1 - core) * half_rows, half_rows), half_in, core_s, core_r, sibling
    )
    core_copy.start()

    labels_copy.wait()
    label_row = labels[...]
    onehot = lax.broadcasted_iota(jnp.int32, (F, rows), 0) == label_row
    before = (
        lax.broadcasted_iota(jnp.int32, (rows, rows), 0)
        < lax.broadcasted_iota(jnp.int32, (rows, rows), 1)
    )
    flags = jnp.where(onehot, 1.0, 0.0)
    rank_all = dot(flags.astype(jnp.bfloat16), jnp.where(before, 1.0, 0.0).astype(jnp.bfloat16))
    rank = jnp.sum(jnp.where(onehot, rank_all, 0.0), axis=0, keepdims=True).astype(jnp.int32)
    amounts = jnp.sum(flags, axis=1, keepdims=True)
    for label in range(F):
        counts_out[label] = jnp.broadcast_to(amounts[label:label + 1, :], (8, LANES))
    slot_of = label_row * slot + rank
    def slot_rows(ref, which):
        return ref.at[pl.ds(pl.multiple_of(which * slot, 16), slot)]

    def row_copy(to, source):
        return remote(
            slot_rows(outgoing, to), slot_rows(received, source), a_s.at[to], a_r.at[source], (c, to)
        )

    def count_copy(to, source):
        return remote(counts_out.at[to], counts_in.at[source], n_s.at[to], n_r.at[source], (c, to))

    def compact(devices):
        places = lax.broadcasted_iota(jnp.int32, (slot, rows), 0)
        picks = [
            jnp.where(places + to * slot == slot_of, 1.0, 0.0).astype(jnp.bfloat16) for to in devices
        ]
        picked = dot(jnp.concatenate(picks, axis=0), emb[...]).astype(jnp.bfloat16)
        for n, to in enumerate(devices):
            slot_rows(outgoing, to)[...] = picked[n * slot:(n + 1) * slot, :]

    compact(lots[0])

    core_copy.wait_recv()
    half[...] = rows_at(acc, core * half_rows, half_rows)[...] + half_in[...]

    def coarse_copy(to, source):
        return remote(
            rows_at(half, to * part_rows, part_rows), coarse_in.at[source],
            coarse_s.at[to], coarse_r.at[source], (to, f),
        )

    for k in range(1, C):
        coarse_copy(coarse_peer(k), c).start()
    for peer in lots[0]:
        row_copy(peer, f).start()
    for peer in peers:
        count_copy(peer, f).start()
    compact(lots[1] + lots[2] + [f])
    slot_rows(received, f)[...] = slot_rows(outgoing, f)[...]
    counts_in[f] = counts_out[f]
    value = rows_at(half, c * part_rows, part_rows)[...]
    for k in range(1, C):
        coarse_copy(coarse_peer(k), coarse_peer(k)).wait_recv()
        value = value + coarse_in[coarse_peer(k)]
    part[...] = value

    def z_copy(to, source):
        return remote(
            rows_at(part, to * piece_rows, piece_rows), z_in.at[source],
            z_s.at[to], z_r.at[source], (c, 2 * to + core),
        )

    for k in range(1, Z):
        z_copy(z_peer(k), z).start()
    value = rows_at(part, z * piece_rows, piece_rows)[...]
    for k in range(1, Z):
        z_copy(z_peer(k), z_peer(k)).wait_recv()
        value = value + z_in[z_peer(k)]

    def piece_start(coarse_id, z_id):
        return core * half_rows + coarse_id * part_rows + z_id * piece_rows

    rows_at(total, piece_start(c, z), piece_rows)[...] = value

    def z_gather(to, source):
        piece = rows_at(total, piece_start(c, source), piece_rows)
        return remote(piece, piece, gz_s.at[to], gz_r.at[source], (c, 2 * to + core))

    def coarse_gather(to, source):
        piece = rows_at(total, piece_start(source, 0), part_rows)
        return remote(piece, piece, gc_s.at[to], gc_r.at[source], (to, f))

    def core_gather(source):
        piece = rows_at(total, source * half_rows, half_rows)
        return remote(piece, piece, gk_s, gk_r, sibling)

    for k in range(1, Z):
        z_gather(z_peer(k), z).start()
    for k in range(1, Z):
        z_gather(z_peer(k), z_peer(k)).wait_recv()
    for k in range(1, C):
        coarse_gather(coarse_peer(k), c).start()
    for peer in lots[1]:
        row_copy(peer, f).start()
    for k in range(1, C):
        coarse_gather(coarse_peer(k), coarse_peer(k)).wait_recv()
    core_gather(core).start()
    for peer in lots[2]:
        row_copy(peer, f).start()

    for k in range(1, F):
        count_copy(fine_peer(k), fine_peer(k)).wait_recv()

    core_gather(1 - core).wait_recv()
    for place, (i, j) in enumerate(pairs):
        block = total[place * LANES:(place + 1) * LANES, :] * (1.0 / row_total)
        if i == j:
            diagonal = (
                lax.broadcasted_iota(jnp.int32, (LANES, LANES), 0)
                == lax.broadcasted_iota(jnp.int32, (LANES, LANES), 1)
            )
            block = block + jnp.where(diagonal, RIDGE, 0.0)
        else:
            full[j * LANES:(j + 1) * LANES, i * LANES:(i + 1) * LANES] = block.T
        full[i * LANES:(i + 1) * LANES, j * LANES:(j + 1) * LANES] = block
    second = full[...]
    norm_scale = jnp.max(jnp.sum(jnp.abs(second), axis=0, keepdims=True), axis=1, keepdims=True)
    root = second * (1.0 / norm_scale)
    identity = jnp.where(
        lax.broadcasted_iota(jnp.int32, (width, width), 0)
        == lax.broadcasted_iota(jnp.int32, (width, width), 1),
        2.25, 0.0,
    )
    root_b = root.astype(jnp.bfloat16)
    square = dot(root_b, root_b)
    outer = (0.0625 * square - 0.5625 * root).astype(jnp.bfloat16)
    inverse = identity - 2.4375 * root + 1.6875 * square + dot(square.astype(jnp.bfloat16), outer)
    whiten[...] = (inverse * (1.0 / jnp.sqrt(norm_scale))).astype(jnp.bfloat16)

    group = LANES // slot
    if group == 1:
        batches = [[f] + lots[0] + lots[1], lots[2]]
    else:
        batches = [[lax.rem(lax.div(f, group) + n, F // group) for n in range(F // group)]]
        for peer in peers:
            row_copy(peer, peer).wait_recv()
    order = sum(batches, [])
    rank_here = lax.broadcasted_iota(jnp.int32, (slot, LANES), 0).astype(jnp.float32)
    diagonal = (
        lax.broadcasted_iota(jnp.int32, (LANES, LANES), 0)
        == lax.broadcasted_iota(jnp.int32, (LANES, LANES), 1)
    )

    def highest(tile):
        return jnp.max(tile.reshape(LANES // 8, 8, LANES), axis=0)

    tops, biases, done = [], [], 0
    for batch in batches:
        if group == 1:
            for block in batch:
                if block is not f:
                    row_copy(block, block).wait_recv()
        arrived = [rows_at(received, block * LANES, LANES)[...] for block in batch]
        white = dot(jnp.concatenate(arrived, axis=0), whiten[...])
        meansq = jnp.mean(white * white, axis=-1, keepdims=True)
        here = (white * lax.rsqrt(width * (meansq + EPS))).astype(jnp.bfloat16)
        end = done + len(batch)
        unit[done * LANES:end * LANES, :] = here
        for block in batch:
            bias = [
                jnp.where(rank_here < counts_in[block * group + m][0:1, :], 0.0, LOW) for m in range(group)
            ]
            biases.append(bias[0] if group == 1 else jnp.concatenate(bias, axis=0))
            tops.append(jnp.full((8, LANES), -1.0, jnp.float32))
        down = lax.dot_general(
            here, unit[0:end * LANES, :], (((1,), (1,)), ((), ())), preferred_element_type=jnp.float32
        )
        for q in range(done, end):
            for t in range(end):
                tile = down[(q - done) * LANES:(q - done + 1) * LANES, t * LANES:(t + 1) * LANES] + biases[q]
                if t == q:
                    tile = jnp.where(diagonal, LOW, tile)
                tops[t] = jnp.maximum(tops[t], highest(tile))
        if done > 0:
            across = lax.dot_general(
                unit[0:done * LANES, :], here, (((1,), (1,)), ((), ())), preferred_element_type=jnp.float32
            )
            for q in range(done):
                for t in range(done, end):
                    tile = across[q * LANES:(q + 1) * LANES, (t - done) * LANES:(t - done + 1) * LANES]
                    tops[t] = jnp.maximum(tops[t], highest(tile + biases[q]))
        done = end
    for n, block in enumerate(order):
        best[block] = jnp.broadcast_to(jnp.max(tops[n], axis=0, keepdims=True), (8, LANES))

    def best_copy(to, source):
        return remote(
            best.at[lax.div(to, group)], returned.at[source], b_s.at[to], b_r.at[source], (c, to)
        )

    for peer in peers:
        best_copy(peer, f).start()
    returned[f] = best[lax.div(f, group)]
    pick = lax.broadcasted_iota(jnp.int32, (LANES, rows), 0) == rank + lax.rem(f * slot, LANES)
    pick = jnp.where(pick, 1.0, 0.0).astype(jnp.bfloat16)
    mine = lax.broadcasted_iota(jnp.int32, (F * 8, rows), 0) == label_row * 8
    for k in range(1, F):
        best_copy(fine_peer(k), fine_peer(k)).wait_recv()
    values = returned[...].reshape(F * 8, LANES)
    high, rest = values.astype(jnp.bfloat16), None
    rest = values - high.astype(jnp.float32)
    middle, low = split_two(rest)
    found = dot(high, pick) + (dot(middle, pick) + dot(low, pick))
    out[...] = jnp.sum(jnp.where(mine, found, 0.0), axis=0, keepdims=True)

    core_copy.wait_send()
    core_gather(core).wait_send()
    for k in range(1, C):
        coarse_copy(coarse_peer(k), c).wait_send()
        coarse_gather(coarse_peer(k), c).wait_send()
    for k in range(1, Z):
        z_copy(z_peer(k), z).wait_send()
        z_gather(z_peer(k), z).wait_send()
    for k in range(1, F):
        row_copy(fine_peer(k), f).wait_send()
        count_copy(fine_peer(k), f).wait_send()
        best_copy(fine_peer(k), f).wait_send()


def per_device(embeddings, labels):
    rows, width = embeddings.shape
    F = lax.axis_size("fine")
    C = lax.axis_size("coarse")
    Z = F // 2
    slot = 2 * rows // F
    slots = F * slot
    blocks = width // LANES
    unit_rows = 8 * C * F
    stack_rows = -(-(blocks * (blocks + 1) // 2 * LANES) // unit_rows) * unit_rows
    half_rows = stack_rows // 2
    part_rows = half_rows // C
    piece_rows = part_rows // Z
    f32, bf16 = jnp.float32, jnp.bfloat16
    dma = pltpu.SemaphoreType.DMA
    best = pl.pallas_call(
        functools.partial(kernel, C, F, slot, stack_rows, rows * F * C),
        out_shape=jax.ShapeDtypeStruct((1, rows), f32),
        in_specs=[pl.BlockSpec(memory_space=pl.ANY)] * 2,
        out_specs=pl.BlockSpec(memory_space=pltpu.VMEM),
        scratch_shapes=[
            pltpu.VMEM((rows, width), bf16),
            pltpu.VMEM((1, rows), jnp.int32),
            pltpu.VMEM((stack_rows, LANES), f32),
            pltpu.VMEM((half_rows, LANES), f32),
            pltpu.VMEM((half_rows, LANES), f32),
            pltpu.VMEM((C, part_rows, LANES), f32),
            pltpu.VMEM((part_rows, LANES), f32),
            pltpu.VMEM((Z, piece_rows, LANES), f32),
            pltpu.VMEM((stack_rows, LANES), f32),
            pltpu.VMEM((slots, width), bf16),
            pltpu.VMEM((slots, width), bf16),
            pltpu.VMEM((F, 8, LANES), f32),
            pltpu.VMEM((F, 8, LANES), f32),
            pltpu.VMEM((width, width), f32),
            pltpu.VMEM((width, width), bf16),
            pltpu.VMEM((slots, width), bf16),
            pltpu.VMEM((slots // LANES, 8, LANES), f32),
            pltpu.VMEM((F, 8, LANES), f32),
            dma, dma,
            dma, dma, dma((C,)), dma((C,)), dma((Z,)), dma((Z,)),
            dma((Z,)), dma((Z,)), dma((C,)), dma((C,)), dma, dma,
            dma((F,)), dma((F,)), dma((F,)), dma((F,)), dma((F,)), dma((F,)),
        ],
        compiler_params=pltpu.CompilerParams(
            collective_id=0, has_side_effects=True, vmem_limit_bytes=(64 * 1024 - 256) * 1024
        ),
    )(embeddings, labels.reshape(1, rows))
    return best.reshape(rows)


def solution(mesh):
    in_specs = (P(("coarse", "fine"), None), P(("coarse", "fine"), None))
    out_specs = P(("coarse", "fine"))
    return jax.shard_map(
        per_device, mesh=mesh, in_specs=in_specs, out_specs=out_specs, check_vma=False
    )
```
